32 devices in a mesh: rep: 4 (over y, x), fsdp: 4 (over z), seq: 2 (over core).
Axes of the slice: x: 2, y: 2, z: 4, core: 2. Of those that a mesh axis runs over, the one named last changes fastest.
Arguments:
- hidden_in: bfloat16 [16384, 1024], P(('rep', 'fsdp', 'seq')), may hold values from -6 to 6
- norm1_gain: float32 [1024], replicated, may hold values from 0.5 to 1.5
- w_z: bfloat16 [1024, 1536], P(('fsdp', 'seq')), may hold values from -0.1875 to 0.1875
- w_xbc: bfloat16 [1024, 1792], P(('fsdp', 'seq')), may hold values from -0.1875 to 0.1875
- w_dt: bfloat16 [1024, 24], P(('fsdp', 'seq')), may hold values from -0.1875 to 0.1875
- conv_w: float32 [4, 1792], replicated, may hold values from -0.6 to 0.6
- conv_b: float32 [1792], replicated, may hold values from -0.5 to 0.5
- dt_bias: float32 [24], replicated, may hold values from -1 to 0.5
- a_log: float32 [24], replicated, may hold values from -6.9 to -3
- d_skip: float32 [24], replicated, may hold values from 0.5 to 1.5
- ssm_gain: float32 [1536], replicated, may hold values from 0.5 to 1.5
- w_ssm_out: bfloat16 [1536, 1024], P(None, ('fsdp', 'seq')), may hold values from -0.15625 to 0.15625
- w_q: bfloat16 [1024, 512], P(('fsdp', 'seq')), may hold values from -0.1875 to 0.1875
- key_weight: bfloat16 [1024, 128], P(('fsdp', 'seq')), may hold values from -0.1875 to 0.1875
- value_weight: bfloat16 [1024, 128], P(('fsdp', 'seq')), may hold values from -0.1875 to 0.1875
- w_o: bfloat16 [512, 1024], P(None, ('fsdp', 'seq')), may hold values from -0.75 to 0.75
- norm2_gain: float32 [1024], replicated, may hold values from 0.5 to 1.5
- w_gate: bfloat16 [1024, 2048], P(('fsdp', 'seq')), may hold values from -0.1875 to 0.1875
- w_up: bfloat16 [1024, 2048], P(('fsdp', 'seq')), may hold values from -0.1875 to 0.1875
- w_down: bfloat16 [2048, 1024], P(None, ('fsdp', 'seq')), may hold values from -0.125 to 0.125
- grad_out: bfloat16 [16384, 1024], P(('rep', 'fsdp', 'seq')), may hold values from -6 to 6
Outputs:
- out_hidden: bfloat16 [16384, 1024], P(('rep', 'fsdp', 'seq'))
- grad_hidden: float32 [16384, 1024], P(('rep', 'fsdp', 'seq'))
- grad_norm1_gain: float32 [1024], replicated
- grad_w_z: float32 [1024, 1536], P(('fsdp', 'seq'))
- grad_w_xbc: float32 [1024, 1792], P(('fsdp', 'seq'))
- grad_w_dt: float32 [1024, 24], P(('fsdp', 'seq'))
- grad_conv_w: float32 [4, 1792], replicated
- grad_conv_b: float32 [1792], replicated
- grad_dt_bias: float32 [24], replicated
- grad_a_log: float32 [24], replicated
- grad_d_skip: float32 [24], replicated
- grad_ssm_gain: float32 [1536], replicated
- grad_w_ssm_out: float32 [1536, 1024], P(None, ('fsdp', 'seq'))
- grad_w_q: float32 [1024, 512], P(('fsdp', 'seq'))
- grad_w_k: float32 [1024, 128], P(('fsdp', 'seq'))
- grad_w_v: float32 [1024, 128], P(('fsdp', 'seq'))
- grad_w_o: float32 [512, 1024], P(None, ('fsdp', 'seq'))
- grad_norm2_gain: float32 [1024], replicated
- grad_w_gate: float32 [1024, 2048], P(('fsdp', 'seq'))
- grad_w_up: float32 [1024, 2048], P(('fsdp', 'seq'))
- grad_w_down: float32 [2048, 1024], P(None, ('fsdp', 'seq'))
The draws below stay inside these ranges and needn't reach their ends.
All inputs are finite; a program needn't handle non-finite values.
Results may differ from the reference program's by a relative error of at most 0.018.
Values may be sent and summed in bfloat16 or wider, within the bound.
No kernel may reach another device: no remote copies, remote signals or barrier semaphores. Data moves between devices by JAX's collectives and lax.ppermute only.
A program may use at most 320 MiB of HBM per device.

```python
import jax
import jax.numpy as jnp
from jax import lax

MODEL_WIDTH = 1024
NH_SSM = 24
HP = 64
E = 1536
NS = 128
KCONV = 4
QUERY_HEADS = 8
KEY_VALUE_HEADS = 2
HEAD_SIZE = 64
FF = 2048
BLOCK = 128
LENGTH = 1024
TOKENS = 16384


def block_scale(stream_key, extent, shards, low, largest):
    level = 1.0
    for dim, shards_of in shards:
        heights = jax.random.uniform(jax.random.fold_in(jax.random.fold_in(stream_key, 6), dim), (shards_of,), jnp.float32, low / len(shards), largest / len(shards))
        level = level * jnp.repeat(jnp.exp(heights), extent[dim] // shards_of).reshape((-1,) + (1,) * (len(extent) - 1 - dim))
    return level


def centred(rng, shape, deviation, limit, cuts=(), kind=jnp.bfloat16):
    level = block_scale(rng, shape, cuts, -0.22, 0.18) if cuts else 1.0
    drawn = jax.random.normal(rng, shape, jnp.float32) * deviation * level
    return jnp.minimum(jnp.maximum(drawn, -limit), limit).astype(kind)


def setup_inputs(seed: int = 0) -> dict:
    seeds = jax.random.split(jax.random.key(seed), 22)
    hidden_in = centred(seeds[0], (TOKENS, MODEL_WIDTH), 1.0, 6.0, ((0, 32),))
    norm1_gain = jnp.clip(1.0 + 0.1 * jax.random.normal(seeds[1], (MODEL_WIDTH,), jnp.float32), 0.5, 1.5)
    w_z = centred(seeds[2], (MODEL_WIDTH, E), MODEL_WIDTH ** -0.5, 0.1875, ((0, 8),))
    w_xbc = centred(seeds[3], (MODEL_WIDTH, E + 2 * NS), MODEL_WIDTH ** -0.5, 0.1875, ((0, 8),))
    w_dt = centred(seeds[4], (MODEL_WIDTH, NH_SSM), MODEL_WIDTH ** -0.5, 0.1875, ((0, 8),))
    conv_w = jnp.clip(jax.random.uniform(seeds[5], (KCONV, E + 2 * NS), jnp.float32, -0.6, 0.6), -0.6, 0.6)
    conv_b = jnp.clip(jax.random.uniform(seeds[6], (E + 2 * NS,), jnp.float32, -0.5, 0.5), -0.5, 0.5)
    dt_bias = jnp.clip(jax.random.uniform(seeds[7], (NH_SSM,), jnp.float32, -1.0, 0.5), -1.0, 0.5)
    a_log = jnp.clip(jax.random.uniform(seeds[8], (NH_SSM,), jnp.float32, -6.9, -3.0), -6.9, -3.0)
    d_skip = jnp.clip(jax.random.uniform(seeds[9], (NH_SSM,), jnp.float32, 0.5, 1.5), 0.5, 1.5)
    ssm_gain = jnp.clip(1.0 + 0.1 * jax.random.normal(seeds[10], (E,), jnp.float32), 0.5, 1.5)
    w_ssm_out = centred(seeds[11], (E, MODEL_WIDTH), E ** -0.5, 0.15625, ((1, 8),))
    w_q = centred(seeds[12], (MODEL_WIDTH, QUERY_HEADS * HEAD_SIZE), MODEL_WIDTH ** -0.5, 0.1875, ((0, 8),))
    key_weight = centred(seeds[13], (MODEL_WIDTH, KEY_VALUE_HEADS * HEAD_SIZE), MODEL_WIDTH ** -0.5, 0.1875, ((0, 8),))
    value_weight = centred(seeds[14], (MODEL_WIDTH, KEY_VALUE_HEADS * HEAD_SIZE), MODEL_WIDTH ** -0.5, 0.1875, ((0, 8),))
    w_o = centred(seeds[15], (QUERY_HEADS * HEAD_SIZE, MODEL_WIDTH), HEAD_SIZE ** -0.5, 0.75, ((1, 8),))
    norm2_gain = jnp.clip(1.0 + 0.1 * jax.random.normal(seeds[16], (MODEL_WIDTH,), jnp.float32), 0.5, 1.5)
    w_gate = centred(seeds[17], (MODEL_WIDTH, FF), MODEL_WIDTH ** -0.5, 0.1875, ((0, 8),))
    w_up = centred(seeds[18], (MODEL_WIDTH, FF), MODEL_WIDTH ** -0.5, 0.1875, ((0, 8),))
    w_down = centred(seeds[19], (FF, MODEL_WIDTH), FF ** -0.5, 0.125, ((1, 8),))
    grad_out = centred(seeds[20], (TOKENS, MODEL_WIDTH), 1.0, 6.0, ((0, 32),))
    return dict(hidden_in=hidden_in, norm1_gain=norm1_gain, w_z=w_z, w_xbc=w_xbc, w_dt=w_dt, conv_w=conv_w, conv_b=conv_b, dt_bias=dt_bias, a_log=a_log, d_skip=d_skip, ssm_gain=ssm_gain, w_ssm_out=w_ssm_out, w_q=w_q, key_weight=key_weight, value_weight=value_weight, w_o=w_o, norm2_gain=norm2_gain, w_gate=w_gate, w_up=w_up, w_down=w_down, grad_out=grad_out)


@jax.custom_vjp
def low(v):
    return lax.optimization_barrier(v.astype(jnp.bfloat16)).astype(jnp.float32)

@jax.custom_vjp
def low_back(v):
    return v

def low_keep(v):
    return (low(v), None)

def low_pass(kept, grad):
    return (grad,)

def back_keep(v):
    return (v, None)

def back_low(kept, grad):
    return (low(grad),)
low.defvjp(low_keep, low_pass)
low_back.defvjp(back_keep, back_low)
HIGH = lax.Precision.HIGHEST
EPS = 1e-06
ROPE_BASE = 10000.0

def matrix_product(left_side, right_side):
    return jnp.dot(left_side, right_side, precision=HIGH, preferred_element_type=jnp.float32)

def rms_gain(values, gain):
    return values * lax.rsqrt(lax.optimization_barrier(jnp.mean(values * values, axis=-1, keepdims=True)) + EPS) * gain

def rotate(values, positions):
    half_dim = values.shape[-1] // 2
    frequency = ROPE_BASE ** (-jnp.arange(half_dim, dtype=jnp.float32) / half_dim)
    angles = positions.astype(jnp.float32)[:, None] * frequency[None, :]
    cosine = jnp.cos(angles)[:, None, :]
    sine_part = jnp.sin(angles)[:, None, :]
    first_half = values[..., :half_dim]
    second_half = values[..., half_dim:]
    return jnp.concatenate([first_half * cosine - second_half * sine_part, second_half * cosine + first_half * sine_part], axis=-1)

def conv_piece(extended, conv_w, conv_b, dt_raw, dt_bias, a_log):
    number_of_rows = dt_raw.shape[0]
    total = conv_b[None, :]
    for offset in range(KCONV):
        total = total + conv_w[offset][None, :] * extended[offset:offset + number_of_rows]
    active = jax.nn.silu(total)
    inner = NH_SSM * HP
    values = active[:, :inner].reshape(number_of_rows, NH_SSM, HP)
    b_matrix = active[:, inner:inner + NS]
    c_matrix = active[:, inner + NS:]
    step_size = jax.nn.softplus(dt_raw + dt_bias[None, :])
    log_decay = -step_size * jnp.exp(a_log)[None, :]
    return (values, b_matrix, c_matrix, step_size, log_decay)

def ssd_block(carried, inputs_block):
    values, b_matrix, c_matrix, step_size, log_decay = inputs_block
    number_of_rows = values.shape[0]
    running = jnp.cumsum(log_decay, axis=0)
    causal = (jnp.arange(number_of_rows)[:, None] >= jnp.arange(number_of_rows)[None, :])[:, :, None]
    spread = jnp.where(causal, running[:, None, :] - running[None, :, :], 0.0)
    decay = jnp.where(causal, jnp.exp(spread), 0.0)
    inner_cb = jnp.dot(c_matrix, b_matrix.T, precision=HIGH, preferred_element_type=jnp.float32)
    mixing = decay * inner_cb[:, :, None] * step_size[None, :, :]
    within = jnp.einsum('tsh,shp->thp', mixing, values, precision=HIGH)
    from_state = jnp.einsum('tn,hpn->thp', c_matrix, carried, precision=HIGH) * jnp.exp(running)[:, :, None]
    last_row = running[-1]
    weights_tail = jnp.exp(last_row[None, :] - running) * step_size
    new_state = carried * jnp.exp(last_row)[:, None, None] + jnp.einsum('sh,shp,sn->hpn', weights_tail, values, b_matrix, precision=HIGH)
    return (new_state, within + from_state)

def ssd_scan(values, b_matrix, c_matrix, step_size, log_decay):
    number_of_rows = values.shape[0]
    block_count = number_of_rows // BLOCK
    blocks = (values.reshape(block_count, BLOCK, NH_SSM, HP), b_matrix.reshape(block_count, BLOCK, NS), c_matrix.reshape(block_count, BLOCK, NS), step_size.reshape(block_count, BLOCK, NH_SSM), log_decay.reshape(block_count, BLOCK, NH_SSM))
    initial = jnp.zeros((NH_SSM, HP, NS), jnp.float32)
    final_state, outputs = lax.scan(jax.checkpoint(ssd_block), initial, blocks)
    return (outputs.reshape(number_of_rows, NH_SSM, HP), final_state)

def attention(query_rows, keys, values_kv, query_pos, key_pos):
    grouped_heads = query_rows.reshape(query_rows.shape[0], KEY_VALUE_HEADS, QUERY_HEADS // KEY_VALUE_HEADS, HEAD_SIZE)
    scores = jnp.einsum('tgjd,sgd->gjts', grouped_heads, keys, precision=HIGH) * HEAD_SIZE ** (-0.5)
    scores = low_back(scores)
    allowed = key_pos[None, :] <= query_pos[:, None]
    scores = jnp.where(allowed[None, None], scores, -1e+30)
    peak = lax.optimization_barrier(jnp.max(scores, axis=-1, keepdims=True))
    raised = jnp.exp(scores - peak)
    probs = low(raised / lax.optimization_barrier(jnp.sum(raised, axis=-1, keepdims=True)))
    mixed = jnp.einsum('gjts,sgd->tgjd', probs, values_kv, precision=HIGH)
    return mixed.reshape(query_rows.shape[0], QUERY_HEADS * HEAD_SIZE)

def seq_layer(inputs, weights):
    norm1_gain, w_z, w_xbc, w_dt, conv_w, conv_b, dt_bias, a_log, d_skip, ssm_gain, w_ssm_out, w_q, key_weight, value_weight, w_o, norm2_gain, w_gate, w_up, w_down = weights
    number_of_rows = inputs.shape[0]
    positions = jnp.arange(number_of_rows, dtype=jnp.int32)
    first_normed = low(rms_gain(inputs, norm1_gain))
    gate_z = low_back(matrix_product(first_normed, w_z))
    conv_in = low_back(low(matrix_product(first_normed, w_xbc)))
    dt_raw = low_back(matrix_product(first_normed, w_dt))
    query_raw = low_back(matrix_product(first_normed, w_q)).reshape(number_of_rows, QUERY_HEADS, HEAD_SIZE)
    key_unrotated = low_back(matrix_product(first_normed, key_weight)).reshape(number_of_rows, KEY_VALUE_HEADS, HEAD_SIZE)
    value_projected = low_back(low(matrix_product(first_normed, value_weight))).reshape(number_of_rows, KEY_VALUE_HEADS, HEAD_SIZE)
    extended = jnp.concatenate([jnp.zeros((KCONV - 1, conv_in.shape[1]), jnp.float32), conv_in], axis=0)
    values, b_matrix, c_matrix, step_size, log_decay = conv_piece(extended, conv_w, conv_b, dt_raw, dt_bias, a_log)
    y_local, final_state = ssd_scan(values, b_matrix, c_matrix, step_size, log_decay)
    y_all = (y_local + d_skip[None, :, None] * values).reshape(number_of_rows, NH_SSM * HP)
    ssm_normed = low(rms_gain(y_all * jax.nn.silu(gate_z), ssm_gain))
    mamba_out = low_back(matrix_product(ssm_normed, w_ssm_out))
    query_rows = low(rotate(query_raw, positions))
    keys = low(rotate(key_unrotated, positions))
    attended = low_back(low(attention(query_rows, keys, value_projected, positions, positions)))
    attn_out = low_back(matrix_product(attended, w_o))
    mid = inputs + mamba_out + attn_out
    normed2 = low(rms_gain(mid, norm2_gain))
    gate_pre = low_back(matrix_product(normed2, w_gate))
    up_pre = low_back(matrix_product(normed2, w_up))
    hidden_act = low(jax.nn.silu(gate_pre) * up_pre)
    ffn_out = low_back(matrix_product(hidden_act, w_down))
    return mid + ffn_out

def reference(hidden_in, norm1_gain, w_z, w_xbc, w_dt, conv_w, conv_b, dt_bias, a_log, d_skip, ssm_gain, w_ssm_out, w_q, key_weight, value_weight, w_o, norm2_gain, w_gate, w_up, w_down, grad_out):
    params = tuple((weight_arg.astype(jnp.float32) for weight_arg in (norm1_gain, w_z, w_xbc, w_dt, conv_w, conv_b, dt_bias, a_log, d_skip, ssm_gain, w_ssm_out, w_q, key_weight, value_weight, w_o, norm2_gain, w_gate, w_up, w_down)))
    sequences = hidden_in.astype(jnp.float32).reshape(-1, LENGTH, MODEL_WIDTH)

    def forward(seq_inputs, weights):
        layer_fn = jax.checkpoint(lambda one_seq: seq_layer(one_seq, weights))
        return lax.map(layer_fn, seq_inputs)
    outputs, pullback = jax.vjp(forward, sequences, params)
    grad_seq, grad_params = pullback(grad_out.astype(jnp.float32).reshape(-1, LENGTH, MODEL_WIDTH))
    g_norm1, g_wz, g_wxbc, g_wdt, g_convw, g_convb, g_dtbias, g_alog, g_dskip, g_ssmgain, g_ssmout, g_wq, g_wk, g_wv, g_wo, g_norm2, g_wgate, g_wup, g_wdown = grad_params
    return (outputs.reshape(-1, MODEL_WIDTH).astype(jnp.bfloat16), grad_seq.reshape(-1, MODEL_WIDTH), g_norm1, g_wz, g_wxbc, g_wdt, g_convw, g_convb, g_dtbias, g_alog, g_dskip, g_ssmgain, g_ssmout, g_wq, g_wk, g_wv, g_wo, g_norm2, g_wgate, g_wup, g_wdown)
```

```python
import functools

import jax
import jax.numpy as jnp
from jax import lax
from jax.experimental import pallas as pl
from jax.experimental.pallas import tpu as pltpu
from jax.sharding import PartitionSpec as P

NH_SSM = 24
HP = 64
NS = 128
KCONV = 4
QUERY_HEADS = 8
KEY_VALUE_HEADS = 2
HEAD_SIZE = 64
BLOCK = 128
INNER = NH_SSM * HP
CONV = INNER + 2 * NS
LANES = 128
PAIRS = NH_SSM // 2

HIGH = lax.Precision.HIGHEST
EPS = 1e-06
ROPE_BASE = 10000.0
SCALE = HEAD_SIZE ** (-0.5)
LOW = jnp.bfloat16
F32 = jnp.float32


def mm(a, b):
    return jnp.dot(a, b, preferred_element_type=F32)


def mm_nt(a, b):
    return lax.dot_general(a, b, (((1,), (1,)), ((), ())), preferred_element_type=F32)


def mm_tn(a, b):
    return lax.dot_general(a, b, (((0,), (0,)), ((), ())), preferred_element_type=F32)


def halves(v):
    top = v.astype(LOW)
    return top, (v - top.astype(F32)).astype(LOW)


def spread(v, heads):
    top, rest = halves(v)
    return mm(top, heads) + mm(rest, heads)


def gather_heads(v, heads):
    top, rest = halves(v)
    return mm_nt(top, heads) + mm_nt(rest, heads)


def lane_halves(shape):
    lane = lax.broadcasted_iota(jnp.int32, shape, len(shape) - 1)
    return lane % LANES < HP


def stacked(pair, left):
    zero = jnp.zeros_like(pair)
    return jnp.concatenate([jnp.where(left, pair, zero), jnp.where(left, zero, pair)], axis=0)


def states_kernel(conv_ref, halo_ref, taps_ref, step_ref, run_ref, heads_ref, pre_ref, end_ref, ext):
    block = pl.program_id(0)

    @pl.when(block == 0)
    def _():
        ext[0:8, :] = halo_ref[...]
        end_ref[...] = jnp.zeros_like(end_ref)

    @pl.when(block > 0)
    def _():
        ext[0:8, :] = ext[BLOCK : BLOCK + 8, :]

    ext[8 : BLOCK + 8, :] = conv_ref[...].astype(F32)
    pre = taps_ref[KCONV : KCONV + 1, :] + jnp.zeros((BLOCK, CONV), F32)
    for j in range(KCONV):
        pre = pre + taps_ref[j : j + 1, :] * ext[5 + j : 5 + j + BLOCK, :]
    pre_ref[...] = pre
    heads = heads_ref[...]
    run = run_ref[...]
    last = run[BLOCK - 1 : BLOCK, :]
    tail = jnp.exp(last - run) * step_ref[...]
    wide = spread(jnp.concatenate([tail, jnp.broadcast_to(jnp.exp(last), (8, LANES))], axis=0), heads)
    inner = pre[:, :INNER]
    x = inner * jax.nn.sigmoid(inner)
    bp = pre[:, INNER : INNER + NS]
    b_low = (bp * jax.nn.sigmoid(bp)).T.astype(LOW)
    weighted = (x * wide[:BLOCK]).astype(LOW)
    end_ref[...] = end_ref[...] * wide[BLOCK : BLOCK + 1] + mm(b_low, weighted)


def mixer_kernel(
    pre_ref, step_ref, run_ref, runt_ref, start_ref, z_ref, gain_ref, skip_ref, heads_ref,
    out_ref, y_ref, sin_ref, sout_ref, state,
):
    block = pl.program_id(0)

    @pl.when(block == 0)
    def _():
        state[...] = start_ref[...]

    heads = heads_ref[...]
    run = run_ref[...]
    runt = runt_ref[...]
    step = step_ref[...]
    pre = pre_ref[...]
    act = pre * jax.nn.sigmoid(pre)
    x = act[:, :INNER]
    b = act[:, INNER : INNER + NS]
    c_low = act[:, INNER + NS :].astype(LOW)
    last = run[BLOCK - 1 : BLOCK, :]
    wide = spread(
        jnp.concatenate(
            [
                step,
                jnp.exp(run),
                jnp.exp(last - run) * step,
                jnp.broadcast_to(jnp.exp(last), (8, LANES)),
            ],
            axis=0,
        ),
        heads,
    )
    x_step = (x * wide[:BLOCK]).astype(LOW)
    old = state[...]
    old_low = old.astype(LOW)
    sin_ref[0] = old_low
    carried = mm(c_low, old_low) * wide[BLOCK : 2 * BLOCK]
    weighted = (x * wide[2 * BLOCK : 3 * BLOCK]).astype(LOW)
    new = old * wide[3 * BLOCK : 3 * BLOCK + 1] + mm(b.T.astype(LOW), weighted)
    state[...] = new
    sout_ref[0] = new.astype(LOW)
    cb = mm_nt(c_low, b.astype(LOW))
    rows = lax.broadcasted_iota(jnp.int32, (BLOCK, BLOCK), 0)
    cols = lax.broadcasted_iota(jnp.int32, (BLOCK, BLOCK), 1)
    causal = rows >= cols
    left = lane_halves((BLOCK, LANES))
    parts = []
    for p in range(PAIRS):
        mixes = []
        for h in (2 * p, 2 * p + 1):
            gap = run[:, h : h + 1] - runt[h : h + 1, :]
            mixes.append((jnp.exp(jnp.where(causal, gap, -1e30)) * cb).astype(LOW))
        pair = x_step[:, p * LANES : (p + 1) * LANES]
        parts.append(mm(jnp.concatenate(mixes, axis=1), stacked(pair, left)))
    y = jnp.concatenate(parts, axis=1) + carried
    y_ref[...] = y
    z = z_ref[...]
    gated = (y + skip_ref[...] * x) * (z * jax.nn.sigmoid(z))
    inv = lax.rsqrt(jnp.mean(gated * gated, axis=-1, keepdims=True) + EPS)
    out_ref[...] = (gated * inv * gain_ref[...]).astype(LOW)


def gate_back_kernel(
    g_ref, y_ref, pre_ref, z_ref, run_ref, gain_ref, skip_ref, heads_ref,
    gy_ref, gz_ref, sums_ref, first_ref,
):
    @pl.when(pl.program_id(0) == 0)
    def _():
        sums_ref[...] = jnp.zeros_like(sums_ref)
        first_ref[...] = jnp.zeros_like(first_ref)

    heads = heads_ref[...]
    run = run_ref[...]
    last = run[BLOCK - 1 : BLOCK, :]
    wide = spread(
        jnp.concatenate([jnp.exp(run), jnp.broadcast_to(jnp.exp(last), (8, LANES))], axis=0), heads
    )
    inner = pre_ref[:, :INNER]
    x = inner * jax.nn.sigmoid(inner)
    cp = pre_ref[:, INNER + NS :]
    c = cp * jax.nn.sigmoid(cp)
    y = y_ref[...] + skip_ref[...] * x
    z = z_ref[...]
    sig = jax.nn.sigmoid(z)
    swish = z * sig
    gated = y * swish
    inv = lax.rsqrt(jnp.mean(gated * gated, axis=-1, keepdims=True) + EPS)
    g = g_ref[...]
    gg = g * gain_ref[...]
    mean = jnp.mean(gg * gated, axis=-1, keepdims=True)
    g_gated = gg * inv - gated * (inv * inv * inv * mean)
    g_y = g_gated * swish
    gz_ref[...] = (g_gated * y * (sig + swish * (1.0 - sig))).astype(LOW)
    gy_ref[...] = g_y.astype(LOW)
    sums_ref[0:1, :] += jnp.sum(g * gated * inv, axis=0, keepdims=True)
    sums_ref[1:2, :] += jnp.sum(g_y * x, axis=0, keepdims=True)
    scaled = (g_y * wide[:BLOCK]).astype(LOW)
    first_ref[...] = first_ref[...] * wide[BLOCK : BLOCK + 1] + mm(c.T.astype(LOW), scaled)


def mixer_back_kernel(
    gy_ref, y_ref, pre_ref, step_ref, run_ref, runt_ref, later_ref, sin_ref, sout_ref,
    conv_ref, before_ref, halo_ref, taps_ref, skip_ref, heads_ref,
    gconv_ref, gtail_ref, rim_ref, gstep_ref, grun_ref, gend_ref, gtaps_ref,
    grad_state, ext, dext,
):
    index = pl.program_id(0)
    count = pl.num_programs(0)

    @pl.when(index == 0)
    def _():
        grad_state[...] = later_ref[...]
        gtaps_ref[...] = jnp.zeros_like(gtaps_ref)
        dext[BLOCK : BLOCK + 8, :] = jnp.zeros((8, CONV), F32)

    @pl.when(index > 0)
    def _():
        dext[BLOCK : BLOCK + 8, :] = dext[0:8, :]

    heads = heads_ref[...]
    run = run_ref[...]
    runt = runt_ref[...]
    step = step_ref[...]
    pre = pre_ref[...]
    sig = jax.nn.sigmoid(pre)
    act = pre * sig
    x = act[:, :INNER]
    b = act[:, INNER : INNER + NS]
    c = act[:, INNER + NS :]
    b_low = b.astype(LOW)
    c_low = c.astype(LOW)
    last = run[BLOCK - 1 : BLOCK, :]
    wide = spread(
        jnp.concatenate(
            [step, jnp.exp(run), jnp.exp(last - run), jnp.broadcast_to(jnp.exp(last), (8, LANES))],
            axis=0,
        ),
        heads,
    )
    step_wide = wide[:BLOCK]
    tail_wide = wide[2 * BLOCK : 3 * BLOCK]
    gy_low = gy_ref[...]
    gy = gy_low.astype(F32)
    x_step = (x * step_wide).astype(LOW)
    later = grad_state[...]
    later_low = later.astype(LOW)
    scaled = (gy * wide[BLOCK : 2 * BLOCK]).astype(LOW)
    weighted = (x * (step_wide * tail_wide)).astype(LOW)
    grad_b = mm_nt(weighted, later_low)
    grad_c = mm_nt(scaled, sin_ref[0])
    from_state = mm(b_low, later_low) * tail_wide
    grad_state[...] = later * wide[3 * BLOCK : 3 * BLOCK + 1] + mm(c.T.astype(LOW), scaled)
    ends = jnp.sum(later * sout_ref[0].astype(F32), axis=0, keepdims=True)
    gend_ref[0] = gather_heads(jnp.broadcast_to(ends, (8, INNER)), heads)
    cbt = mm_nt(b_low, c_low)
    rows = lax.broadcasted_iota(jnp.int32, (BLOCK, BLOCK), 0)
    cols = lax.broadcasted_iota(jnp.int32, (BLOCK, BLOCK), 1)
    left = lane_halves((BLOCK, LANES))
    parts = []
    grad_cb = jnp.zeros((BLOCK, BLOCK), F32)
    for p in range(PAIRS):
        lanes = slice(p * LANES, (p + 1) * LANES)
        gy_stack = stacked(gy_low[:, lanes], left)
        products = mm_nt(gy_stack, x_step[:, lanes])
        mixes = []
        for k, h in enumerate((2 * p, 2 * p + 1)):
            column = jnp.broadcast_to(run[:, h : h + 1], (BLOCK, BLOCK))
            gap = column - runt[h : h + 1, :]
            decay = jnp.exp(jnp.where(rows >= cols, gap, -1e30))
            grad_cb = grad_cb + products[k * BLOCK : (k + 1) * BLOCK] * decay
            decay_t = jnp.exp(jnp.where(cols >= rows, -gap, -1e30))
            mixes.append((decay_t * cbt).astype(LOW))
        parts.append(mm(jnp.concatenate(mixes, axis=1), gy_stack))
    u = jnp.concatenate(parts, axis=1) + from_state
    both = gather_heads(
        jnp.concatenate([gy * y_ref[...], x * u], axis=0), heads
    )
    gstep_ref[...] = both[BLOCK:]
    grun_ref[...] = both[:BLOCK] - step * both[BLOCK:]
    grad_cb_low = grad_cb.astype(LOW)
    grad_c = grad_c + mm(grad_cb_low, b_low)
    grad_b = grad_b + mm(grad_cb.T.astype(LOW), c_low)
    grad_x = u * step_wide + skip_ref[...] * gy
    dpre = jnp.concatenate([grad_x, grad_b, grad_c], axis=1) * (sig + act * (1.0 - sig))
    dext[0:BLOCK, :] = dpre
    k = count - 1 - index
    ext[0:8, :] = jnp.where(k == 0, halo_ref[...], before_ref[BLOCK - 16 :, :].astype(F32)[8:])
    ext[8 : BLOCK + 8, :] = conv_ref[...].astype(F32)
    total = jnp.zeros((BLOCK, CONV), F32)
    for j in range(KCONV):
        total = total + taps_ref[j : j + 1, :] * dext[KCONV - 1 - j : KCONV - 1 - j + BLOCK, :]
        gtaps_ref[j : j + 1, :] += jnp.sum(dpre * ext[5 + j : 5 + j + BLOCK, :], axis=0, keepdims=True)
    gtaps_ref[KCONV : KCONV + 1, :] += jnp.sum(dpre, axis=0, keepdims=True)
    gconv_ref[...] = total.astype(LOW)

    @pl.when(index == 0)
    def _():
        gtail_ref[...] = total[BLOCK - 8 :, :]

    rim_ref[...] = dpre[0:8, :]


def fixed(shape):
    return pl.BlockSpec(shape, lambda i: (0,) * len(shape))


def params(mib):
    return pltpu.CompilerParams(
        dimension_semantics=("arbitrary",), vmem_limit_bytes=mib * 1024 * 1024
    )


def rows_of(width):
    return pl.BlockSpec((BLOCK, width), lambda i: (i, 0))


def mixer_states(conv_low, halo, taps, step, run, heads):
    rows = conv_low.shape[0]
    return pl.pallas_call(
        states_kernel,
        grid=(rows // BLOCK,),
        in_specs=[rows_of(CONV), fixed((8, CONV)), fixed((8, CONV)), rows_of(LANES), rows_of(LANES),
                  fixed((LANES, INNER))],
        out_specs=[rows_of(CONV), fixed((NS, INNER))],
        out_shape=[jax.ShapeDtypeStruct((rows, CONV), F32), jax.ShapeDtypeStruct((NS, INNER), F32)],
        scratch_shapes=[pltpu.VMEM((BLOCK + 8, CONV), F32)],
        compiler_params=params(40),
        name="mixer_states",
    )(conv_low, halo, taps, step, run, heads)


def mixer_forward(pre, step, run, runt, start, z, gain, skip, heads):
    rows = pre.shape[0]
    count = rows // BLOCK
    state_spec = pl.BlockSpec((1, NS, INNER), lambda i: (i, 0, 0))
    return pl.pallas_call(
        mixer_kernel,
        grid=(count,),
        in_specs=[rows_of(CONV), rows_of(LANES), rows_of(LANES), rows_of(LANES), fixed((NS, INNER)),
                  rows_of(INNER), fixed((1, INNER)), fixed((1, INNER)), fixed((LANES, INNER))],
        out_specs=[rows_of(INNER), rows_of(INNER), state_spec, state_spec],
        out_shape=[
            jax.ShapeDtypeStruct((rows, INNER), LOW),
            jax.ShapeDtypeStruct((rows, INNER), F32),
            jax.ShapeDtypeStruct((count, NS, INNER), LOW),
            jax.ShapeDtypeStruct((count, NS, INNER), LOW),
        ],
        scratch_shapes=[pltpu.VMEM((NS, INNER), F32)],
        compiler_params=params(40),
        name="mixer_forward",
    )(pre, step, run, runt, start, z, gain, skip, heads)


def gate_back(g, y, pre, z, run, gain, skip, heads):
    rows = pre.shape[0]
    count = rows // BLOCK

    def back(width):
        return pl.BlockSpec((BLOCK, width), lambda i: (count - 1 - i, 0))

    return pl.pallas_call(
        gate_back_kernel,
        grid=(count,),
        in_specs=[back(INNER), back(INNER), back(CONV), back(INNER), back(LANES), fixed((1, INNER)),
                  fixed((1, INNER)), fixed((LANES, INNER))],
        out_specs=[back(INNER), back(INNER), fixed((8, INNER)), fixed((NS, INNER))],
        out_shape=[
            jax.ShapeDtypeStruct((rows, INNER), LOW),
            jax.ShapeDtypeStruct((rows, INNER), LOW),
            jax.ShapeDtypeStruct((8, INNER), F32),
            jax.ShapeDtypeStruct((NS, INNER), F32),
        ],
        compiler_params=params(40),
        name="gate_back",
    )(g, y, pre, z, run, gain, skip, heads)


def mixer_back(gy, y, pre, step, run, runt, later, s_in, s_out, conv_low, halo, taps, skip, heads):
    rows = pre.shape[0]
    count = rows // BLOCK

    def back(width):
        return pl.BlockSpec((BLOCK, width), lambda i: (count - 1 - i, 0))

    state_spec = pl.BlockSpec((1, NS, INNER), lambda i: (count - 1 - i, 0, 0))
    before = pl.BlockSpec((BLOCK, CONV), lambda i: (jnp.maximum(count - 2 - i, 0), 0))
    return pl.pallas_call(
        mixer_back_kernel,
        grid=(count,),
        in_specs=[back(INNER), back(INNER), back(CONV), back(LANES), back(LANES), back(LANES),
                  fixed((NS, INNER)), state_spec, state_spec, back(CONV), before, fixed((8, CONV)),
                  fixed((8, CONV)), fixed((1, INNER)), fixed((LANES, INNER))],
        out_specs=[back(CONV), fixed((8, CONV)), fixed((8, CONV)), back(LANES), back(LANES),
                   pl.BlockSpec((1, 8, LANES), lambda i: (count - 1 - i, 0, 0)), fixed((8, CONV))],
        out_shape=[
            jax.ShapeDtypeStruct((rows, CONV), LOW),
            jax.ShapeDtypeStruct((8, CONV), F32),
            jax.ShapeDtypeStruct((8, CONV), F32),
            jax.ShapeDtypeStruct((rows, LANES), F32),
            jax.ShapeDtypeStruct((rows, LANES), F32),
            jax.ShapeDtypeStruct((count, 8, LANES), F32),
            jax.ShapeDtypeStruct((8, CONV), F32),
        ],
        scratch_shapes=[
            pltpu.VMEM((NS, INNER), F32),
            pltpu.VMEM((BLOCK + 8, CONV), F32),
            pltpu.VMEM((BLOCK + 8, CONV), F32),
        ],
        compiler_params=params(48),
        name="mixer_back",
    )(gy, y, pre, step, run, runt, later, s_in, s_out, conv_low, conv_low, halo, taps, skip, heads)


def turned(x, cosine, sine):
    half = HEAD_SIZE // 2
    lane = lax.broadcasted_iota(jnp.int32, x.shape, 1)
    other = jnp.where(
        lane % HEAD_SIZE < half, pltpu.roll(x, LANES - half, axis=1), pltpu.roll(x, half, axis=1)
    )
    return x * cosine + other * sine


def group_keys(value, group, left):
    other = pltpu.roll(value, HEAD_SIZE, axis=1)
    return jnp.where(left == (group == 0), value, other).astype(LOW)


def group_rows(value, group):
    turned_over = value.T
    return jnp.where(group == 0, turned_over[:HEAD_SIZE], turned_over[HEAD_SIZE:]).astype(LOW)


def attend_kernel(first_ref, q_ref, cos_ref, sin_ref, kv_ref, out_ref, q_low_ref, norm_ref):
    keys, rows = kv_ref.shape[0], q_ref.shape[0]
    group = pl.program_id(0) // 2
    left = lane_halves((rows, LANES))
    key_at = lax.broadcasted_iota(jnp.int32, (keys, rows), 0)
    query_at = lax.broadcasted_iota(jnp.int32, (keys, rows), 1) + first_ref[0]
    seen = key_at <= query_at
    q = (turned(q_ref[...], cos_ref[...], sin_ref[...]).astype(LOW) * SCALE).astype(LOW)
    q_low_ref[...] = q
    k = group_keys(kv_ref[:, :LANES].astype(F32), group, lane_halves((keys, LANES)))
    vt = group_rows(kv_ref[:, LANES:].astype(F32), group)
    zero = jnp.zeros_like(q)
    parts = []
    norm_ref[...] = jnp.zeros_like(norm_ref)
    for n in range(2):
        mine = jnp.where(left, q, zero) if n == 0 else jnp.where(left, zero, q)
        scores = jnp.where(seen, mm_nt(k, mine), -1e30)
        peak = jnp.max(scores, axis=0, keepdims=True)
        raised = jnp.exp(scores - peak)
        total = jnp.sum(raised, axis=0, keepdims=True)
        probs = (raised * (1.0 / total)).astype(LOW)
        norm_ref[0, n : n + 1, :] = peak + jnp.log(total)
        parts.append(mm(vt, probs))
    out_ref[...] = jnp.concatenate(parts, axis=0).T.astype(LOW)


def attend_back_kernel(
    first_ref, g_ref, q_ref, cos_ref, sin_ref, kv_ref, norm_ref, gq_ref, gkv_ref
):
    keys, rows = kv_ref.shape[0], q_ref.shape[0]
    step = pl.program_id(0)
    group = step // 2
    left = lane_halves((rows, LANES))
    key_left = lane_halves((keys, LANES))
    key_at = lax.broadcasted_iota(jnp.int32, (keys, rows), 0)
    query_at = lax.broadcasted_iota(jnp.int32, (keys, rows), 1) + first_ref[0]
    seen = key_at <= query_at
    q = q_ref[...]
    g = g_ref[...].astype(LOW)
    k_wide = kv_ref[:, :LANES].astype(F32)
    k = group_keys(k_wide, group, key_left)
    kt = group_rows(k_wide, group)
    v = group_keys(kv_ref[:, LANES:].astype(F32), group, key_left)
    zero = jnp.zeros_like(q)
    parts = []
    gk = jnp.zeros((keys, LANES), F32)
    gv = jnp.zeros((keys, LANES), F32)
    for n in range(2):
        mine = jnp.where(left, q, zero) if n == 0 else jnp.where(left, zero, q)
        grad = jnp.where(left, g, zero) if n == 0 else jnp.where(left, zero, g)
        scores = jnp.where(seen, mm_nt(k, mine), -1e30)
        probs = jnp.exp(scores - norm_ref[0, n : n + 1, :])
        g_probs = mm_nt(v, grad)
        inner = jnp.sum(probs * g_probs, axis=0, keepdims=True)
        g_scores = (probs * (g_probs - inner)).astype(LOW)
        gk = gk + mm(g_scores, mine)
        gv = gv + mm(probs.astype(LOW), grad)
        parts.append(mm(kt, g_scores))
    grad_q = jnp.concatenate(parts, axis=0).T * SCALE
    gq_ref[...] = turned(grad_q, cos_ref[...], -sin_ref[...]).astype(LOW)
    here = key_left == (group == 0)

    @pl.when(step == 0)
    def _():
        gkv_ref[...] = jnp.zeros_like(gkv_ref)

    for n, value in enumerate((gk, gv)):
        both = value + pltpu.roll(value, HEAD_SIZE, axis=1)
        gkv_ref[:, n * LANES : (n + 1) * LANES] += jnp.where(here, both, 0.0)


def attend(first, proj, q_at, cosine, sine, kv):
    rows, keys = proj.shape[0], kv.shape[0]
    count = QUERY_HEADS // 2
    column = pl.BlockSpec((rows, LANES), lambda i: (0, i))
    low = jax.ShapeDtypeStruct((rows, QUERY_HEADS * HEAD_SIZE), LOW)
    return pl.pallas_call(
        attend_kernel,
        grid=(count,),
        in_specs=[
            pl.BlockSpec(memory_space=pltpu.SMEM),
            pl.BlockSpec((rows, LANES), lambda i: (0, q_at // LANES + i)),
            fixed((rows, LANES)),
            fixed((rows, LANES)),
            fixed((keys, 2 * LANES)),
        ],
        out_specs=[column, column, pl.BlockSpec((1, 8, rows), lambda i: (i, 0, 0))],
        out_shape=[low, low, jax.ShapeDtypeStruct((count, 8, rows), F32)],
        compiler_params=params(48),
        name="attend",
    )(first, proj, cosine, sine, kv)


def attend_back(first, g, g_at, q, cosine, sine, kv, norm):
    rows, keys = q.shape[0], kv.shape[0]
    count = QUERY_HEADS // 2
    column = pl.BlockSpec((rows, LANES), lambda i: (0, i))
    return pl.pallas_call(
        attend_back_kernel,
        grid=(count,),
        in_specs=[
            pl.BlockSpec(memory_space=pltpu.SMEM),
            pl.BlockSpec((rows, LANES), lambda i: (0, g_at // LANES + i)),
            column,
            fixed((rows, LANES)),
            fixed((rows, LANES)),
            fixed((keys, 2 * LANES)),
            pl.BlockSpec((1, 8, rows), lambda i: (i, 0, 0)),
        ],
        out_specs=[column, fixed((keys, 2 * LANES))],
        out_shape=[
            jax.ShapeDtypeStruct(q.shape, LOW),
            jax.ShapeDtypeStruct((keys, 2 * LANES), F32),
        ],
        compiler_params=params(48),
        name="attend_back",
    )(first, g, q, cosine, sine, kv, norm)


def trade(value, axis, bit):
    count = lax.axis_size(axis)
    return lax.ppermute(value, axis, [(i, i ^ bit) for i in range(count)])


def shifted(value, axis, by):
    count = lax.axis_size(axis)
    return lax.ppermute(value, axis, [(i, (i + by) % count) for i in range(count)])


def from_behind(value, axis, by):
    count = lax.axis_size(axis)
    pairs = [(i, i + by) for i in range(count) if 0 <= i + by < count]
    return lax.ppermute(value, axis, pairs)


def bits_of(count, flip):
    bits = [1 << k for k in range(count.bit_length() - 1)]
    return bits[::-1] if flip else bits


class Flow:
    def __init__(self, steps):
        self.steps, self.value = steps, None
        self.pending = next(steps)

    def advance(self, arrived):
        try:
            self.pending = self.steps.send(arrived)
        except StopIteration as end:
            self.pending, self.value = [], end.value


def tick(flows, values):
    arrived, values = lax.optimization_barrier(([f.pending for f in flows], values))
    for flow, got in zip(flows, arrived):
        flow.advance(got)
    return values


def sharing(own, split):
    reps = lax.axis_size("rep")
    held = [{0: own[:, :split]}, {0: own[:, split:]}]
    for bits in zip(bits_of(reps, False), bits_of(reps, True)):
        orders = [sorted(h) for h in held]
        sent = [jnp.concatenate([h[b] for b in order], axis=0) for h, order in zip(held, orders)]
        got = yield [trade(v, "rep", bit) for v, bit in zip(sent, bits)]
        for h, order, bit, value in zip(held, orders, bits, got):
            value = value.reshape(len(order), -1, value.shape[1])
            for k, b in enumerate(order):
                h[b ^ bit] = value[k]
    return [[h[b] for b in range(reps)] for h in held]


def gathering(shard, split):
    reps, depth = lax.axis_size("rep"), lax.axis_size("fsdp")
    rep = lax.axis_index("rep")
    unit = shard.shape[0] // reps
    quarters = [lax.dynamic_slice_in_dim(shard, (rep ^ b) * unit, unit, 0) for b in range(reps)]
    far = yield [shifted(quarters[0], "fsdp", s) for s in range(1, depth)]
    shared = yield from sharing(jnp.concatenate(far, axis=0), split)
    sides = []
    for side, columns in zip(shared, (slice(0, split), slice(split, None))):
        parts = [part for b in range(reps) for part in (quarters[b][:, columns], side[b])]
        sides.append(jnp.concatenate(parts, axis=0))
    own = jnp.concatenate(sides, axis=1)
    return [own] + (yield [trade(own, "seq", a) for a in range(1, lax.axis_size("seq"))])


def reducing(left, right, split):
    seqs, reps, depth = lax.axis_size("seq"), lax.axis_size("rep"), lax.axis_size("fsdp")
    part = left.shape[1] // seqs
    sent = [mm_tn(left[:, a * part : (a + 1) * part], right).astype(LOW) for a in range(1, seqs)]
    got = yield [trade(value, "seq", a + 1) for a, value in enumerate(sent)]
    total = mm_tn(left[:, :part], right)
    for value in got:
        total = total + value.astype(F32)
    total = total.reshape(reps, part // reps, right.shape[1])
    held = [{b: total[b, :, :split] for b in range(reps)}, {b: total[b, :, split:] for b in range(reps)}]
    for bits in zip(bits_of(reps, False), bits_of(reps, True)):
        away = [sorted(b for b in h if b & bit) for h, bit in zip(held, bits)]
        sent = [jnp.concatenate([h[b] for b in bs], axis=0).astype(LOW) for h, bs in zip(held, away)]
        got = yield [trade(v, "rep", bit) for v, bit in zip(sent, bits)]
        for n, (h, bs, bit, value) in enumerate(zip(held, away, bits, got)):
            value = value.reshape(len(bs), -1, value.shape[1])
            held[n] = {b: h[b] + value[bs.index(b ^ bit)].astype(F32) for b in h if not b & bit}
    mine = jnp.concatenate([held[0][0], held[1][0]], axis=1).reshape(depth, -1, right.shape[1])
    got = yield [shifted(mine[s].astype(LOW), "fsdp", -s) for s in range(1, depth)]
    total = mine[0]
    for value in got:
        total = total + value.astype(F32)
    return total.astype(LOW)


def completing(own, split):
    left, right = yield from sharing(own, split)
    rep = lax.axis_index("rep")
    sides = []
    for side in (left, right):
        stack = jnp.stack(side)
        ordered = [lax.dynamic_index_in_dim(stack, rep ^ q, 0, False) for q in range(len(side))]
        sides.append(jnp.concatenate(ordered, axis=0))
    return jnp.concatenate(sides, axis=1).astype(F32)


def summing(value):
    for axis in ("seq", "rep", "fsdp"):
        for bit in bits_of(lax.axis_size(axis), False):
            (got,) = yield [trade(value, axis, bit)]
            value = value + got
    return value


def into(x, weight):
    part = x.shape[1] // len(weight)
    return sum(mm(x[:, a * part : (a + 1) * part], w) for a, w in enumerate(weight))


def out_of(pairs):
    count = len(pairs[0][1])
    return jnp.concatenate([sum(mm_nt(g, weight[a]) for g, weight in pairs) for a in range(count)], axis=1)


def rms_back(g, v, gain):
    r = lax.rsqrt(jnp.mean(v * v, axis=-1, keepdims=True) + EPS)
    scaled = g * gain
    mean = jnp.mean(scaled * v, axis=-1, keepdims=True)
    return r * scaled - v * (r * r * r * mean), jnp.sum(g * v * r, axis=0, keepdims=True)


def rms_gain(v, gain):
    return v * lax.rsqrt(jnp.mean(v * v, axis=-1, keepdims=True) + EPS) * gain


def swap_halves(x):
    half = HEAD_SIZE // 2
    pieces = []
    for start in range(0, x.shape[1], HEAD_SIZE):
        pieces += [x[:, start + half : start + HEAD_SIZE], x[:, start : start + half]]
    return jnp.concatenate(pieces, axis=1)


def body(
    hidden_in, norm1_gain, w_z, w_xbc, w_dt, conv_w, conv_b, dt_bias, a_log, d_skip, ssm_gain, w_ssm_out,
    w_q, key_weight, value_weight, w_o, norm2_gain, w_gate, w_up, w_down, grad_out,
):
    rows, width = hidden_in.shape
    seqs, reps, depth = lax.axis_size("seq"), lax.axis_size("rep"), lax.axis_size("fsdp")
    core, rep, deep = lax.axis_index("seq"), lax.axis_index("rep"), lax.axis_index("fsdp")
    shard = w_z.shape[0]
    unit = shard // reps
    blocks = rows // BLOCK

    place = jnp.arange(width, dtype=jnp.int32)
    u, s = place % unit, place // unit % depth
    b, a = place // (unit * depth) % reps, place // (unit * depth * reps)
    source = ((((deep - s) % depth) * seqs + (core ^ a)) * reps + (rep ^ b)) * unit + u
    order = (place[:, None] == source[None, :]).astype(LOW)

    pack_a = jnp.concatenate(
        [w_z, w_q, key_weight, value_weight, w_xbc, jnp.pad(w_dt, ((0, 0), (0, LANES - NH_SSM)))], axis=1
    )
    q_at, k_at, v_at, conv_at, dt_at = INNER, INNER + 512, INNER + 640, INNER + 768, INNER + 768 + CONV
    flow_a = Flow(gathering(pack_a, 2176))
    pack_b = jnp.concatenate([w_ssm_out, w_o], axis=0).T
    pack_c = jnp.concatenate([w_gate, w_up], axis=1)
    pack_d = w_down.T
    gains = jnp.dot(
        jnp.concatenate([norm1_gain[None], norm2_gain[None], jnp.zeros((6, width), F32)], axis=0),
        order.astype(F32), precision=HIGH,
    )
    gain_1, gain_2 = gains[0:1], gains[1:2]
    inputs = mm(hidden_in, order)
    upstream_low = mm(grad_out, order).astype(LOW)
    normed_1 = rms_gain(inputs, gain_1).astype(LOW)
    inputs = inputs.astype(LOW)
    pack_b, pack_c, pack_d, inputs, upstream_low, normed_1, order = tick(
        [flow_a], (pack_b, pack_c, pack_d, inputs, upstream_low, normed_1, order)
    )
    flow_b = Flow(gathering(pack_b, 1024))

    lanes = jnp.arange(LANES, dtype=jnp.int32)
    half = HEAD_SIZE // 2
    frequency = ROPE_BASE ** (-(lanes % half).astype(F32) / half)
    positions = core * rows + jnp.arange(rows, dtype=jnp.int32)
    angles = positions.astype(F32)[:, None] * frequency[None, :]
    cosine = jnp.cos(angles)
    sine = jnp.sin(angles) * jnp.where(lanes % HEAD_SIZE < half, -1.0, 1.0)[None, :]
    heads = (jnp.arange(LANES)[:, None] == jnp.arange(INNER)[None, :] // HP).astype(LOW)
    taps = jnp.concatenate([conv_w, conv_b[None], jnp.zeros((3, CONV), F32)], axis=0)
    skip = jnp.repeat(d_skip, HP)[None, :]
    gain_s = ssm_gain[None, :]
    pack_c, pack_d, cosine, sine, heads, taps, skip = tick(
        [flow_a], (pack_c, pack_d, cosine, sine, heads, taps, skip)
    )
    flow_c = Flow(gathering(pack_c, 2048))
    pack_d = tick([flow_a, flow_b], pack_d)
    normed_1, pack_d = tick([flow_a, flow_b], (normed_1, pack_d))
    full_a = flow_a.value
    flow_d = Flow(gathering(pack_d, 1024))

    proj = into(normed_1, full_a)
    conv_low = proj[:, conv_at:dt_at].astype(LOW)
    dt_raw = proj[:, dt_at:]
    k_raw = proj[:, k_at:v_at]
    k_low = (k_raw * cosine + swap_halves(k_raw) * sine).astype(LOW)
    kv = lax.all_gather(
        jnp.concatenate([k_low, proj[:, v_at:conv_at].astype(LOW)], axis=1), "seq", axis=0, tiled=True
    )
    halo = from_behind(conv_low[rows - 8 :], "seq", 1).astype(F32)
    step = jax.nn.softplus(dt_raw[:, :NH_SSM] + dt_bias[None, :])
    rate = jnp.exp(a_log)[None, :]
    log_decay = -step * rate
    lower = (jnp.arange(BLOCK)[:, None] >= jnp.arange(BLOCK)[None, :]).astype(F32)
    pad = ((0, 0), (0, LANES - NH_SSM))
    step_pad = jnp.pad(step, pad)
    run = jnp.einsum(
        "ts,ksh->kth", lower, jnp.pad(log_decay, pad).reshape(blocks, BLOCK, LANES), precision=HIGH
    )
    runt = jnp.swapaxes(run, 1, 2).reshape(rows, LANES)
    whole_decay = jnp.exp(jnp.sum(run[:, BLOCK - 1, :NH_SSM], axis=0))
    decay_wide = jnp.repeat(whole_decay, HP)[None, :]
    run = run.reshape(rows, LANES)
    pre, end_state = mixer_states(conv_low, halo, taps, step_pad, run, heads)
    kv, pre, end_state, proj = tick([flow_b, flow_c], (kv, pre, end_state, proj))

    incoming = jnp.zeros_like(end_state)
    for _ in range(seqs - 1):
        incoming = from_behind((end_state + decay_wide * incoming).astype(LOW), "seq", 1).astype(F32)
    start = (core * rows).astype(jnp.int32)[None]
    attended, q_low, norms = attend(start, proj, q_at, cosine, sine, kv)
    incoming, attended, proj = tick([flow_b, flow_c], (incoming, attended, proj))
    full_b = flow_b.value

    ssm_low, y, s_in, s_out = mixer_forward(
        pre, step_pad, run, runt, incoming, proj, gain_s, skip, heads
    )
    both = jnp.concatenate([ssm_low, attended], axis=1)
    both, y, s_in, s_out = tick([flow_c, flow_d], (both, y, s_in, s_out))

    mid = inputs.astype(F32) + out_of([(both, full_b)])
    normed_2 = rms_gain(mid, gain_2).astype(LOW)
    mid, normed_2 = tick([flow_c, flow_d], (mid, normed_2))
    full_c = flow_c.value

    gate_up = into(normed_2, full_c)
    hidden = gate_up.shape[1] // 2
    gate_pre, up_pre = gate_up[:, :hidden], gate_up[:, hidden:]
    sig = jax.nn.sigmoid(gate_pre)
    swish = gate_pre * sig
    act = (swish * up_pre).astype(LOW)
    act, gate_up = tick([flow_d], (act, gate_up))
    act, gate_up = tick([flow_d], (act, gate_up))
    full_d = flow_d.value

    sum_d = Flow(reducing(upstream_low, act, 1024))
    gate_pre, up_pre = gate_up[:, :hidden], gate_up[:, hidden:]
    sig = jax.nn.sigmoid(gate_pre)
    swish = gate_pre * sig
    g_act = into(upstream_low, full_d)
    g_gate_up = jnp.concatenate(
        [(g_act * up_pre * (sig + swish * (1.0 - sig))).astype(LOW), (g_act * swish).astype(LOW)], axis=1
    )
    g_gate_up, act = tick([sum_d], (g_gate_up, act))

    sum_c = Flow(reducing(normed_2, g_gate_up, 2048))
    g_n2 = out_of([(g_gate_up, full_c)])
    upstream = upstream_low.astype(F32)
    g_add, g_gain_2 = rms_back(g_n2, mid, gain_2)
    g_mid = upstream + g_add
    g_low = g_mid.astype(LOW)
    g_both = into(g_low, full_b)
    g_low, g_both, g_mid = tick([sum_d, sum_c], (g_low, g_both, g_mid))

    sum_b = Flow(reducing(g_low, both, 1024))
    gy, gz, gate_sums, first_grad = gate_back(g_both, y, pre, proj, run, gain_s, skip, heads)
    later = jnp.zeros_like(first_grad)
    for _ in range(seqs - 1):
        later = from_behind((first_grad + decay_wide * later).astype(LOW), "seq", -1).astype(F32)
    g_q, g_kv = attend_back(start, g_both, INNER, q_low, cosine, sine, kv, norms)
    gy, gz, later, g_q, g_kv = tick([sum_d, sum_c, sum_b], (gy, gz, later, g_q, g_kv))

    own_kv = lax.dynamic_slice_in_dim(g_kv, core * rows, rows, 0)
    for shift in range(1, seqs):
        part = lax.dynamic_slice_in_dim(g_kv, ((core + shift) % seqs) * rows, rows, 0).astype(LOW)
        own_kv = own_kv + shifted(part, "seq", shift).astype(F32)
    g_k = own_kv[:, :LANES]
    g_k_low = (g_k * cosine - swap_halves(g_k) * sine).astype(LOW)
    g_second = jnp.concatenate([gz, g_q, g_k_low, own_kv[:, LANES:].astype(LOW)], axis=1)
    out_perm = (mid + out_of([(act, full_d)])).astype(LOW)
    out_hidden = mm_nt(out_perm, order).astype(LOW)
    g_second, gy, out_hidden = tick([sum_d, sum_c, sum_b], (g_second, gy, out_hidden))

    sum_a1 = Flow(reducing(normed_1, g_second, 1152))
    g_conv, g_tail, rim, g_step, g_run, g_end, g_taps = mixer_back(
        gy, y, pre, step_pad, run, runt, later, s_in, s_out, conv_low, halo, taps, skip, heads
    )
    g_conv, g_tail, rim, g_step, g_run, g_end, g_taps = tick(
        [sum_c, sum_b, sum_a1], (g_conv, g_tail, rim, g_step, g_run, g_end, g_taps)
    )
    rim_back = jnp.concatenate(
        [
            sum(
                conv_w[j][None] * rim[t + KCONV - 1 - j : t + KCONV - j]
                for j in range(KCONV)
                if t + KCONV - 1 - j >= 0
            )
            for t in range(1 - KCONV, 0)
        ],
        axis=0,
    )
    rim_back = from_behind(rim_back, "seq", -1)
    tail = jnp.concatenate([g_tail[: 9 - KCONV], g_tail[9 - KCONV :] + rim_back], axis=0).astype(LOW)
    g_conv = lax.dynamic_update_slice(g_conv, tail, (rows - 8, 0))
    g_log = jnp.einsum("ts,kth->ksh", lower, g_run.reshape(blocks, BLOCK, LANES), precision=HIGH)
    g_log = (g_log + g_end[:, 0:1, :]).reshape(rows, LANES)[:, :NH_SSM]
    g_step = g_step[:, :NH_SSM] - g_log * rate
    g_dt = g_step * jax.nn.sigmoid(dt_raw[:, :NH_SSM] + dt_bias[None, :])
    g_a_log = jnp.sum(g_log * log_decay, axis=0)
    g_dt_bias = jnp.sum(g_dt, axis=0)
    g_first = jnp.concatenate([g_conv, jnp.pad(g_dt, pad).astype(LOW)], axis=1)
    sum_a2 = Flow(reducing(normed_1, g_first, 1024))
    g_n1 = out_of([(g_second, [w[:, :conv_at] for w in full_a]), (g_first, [w[:, conv_at:] for w in full_a])])
    g_n1, g_mid = tick([sum_b, sum_a1, sum_a2], (g_n1, g_mid))

    done = jnp.concatenate([sum_d.value, sum_c.value, sum_b.value], axis=1)
    out_1 = Flow(completing(done, 4096))
    inputs_wide = inputs.astype(F32)
    g_add, g_gain_1 = rms_back(g_n1, inputs_wide, gain_1)
    g_hidden = g_mid + g_add
    top, rest = halves(g_hidden)
    grad_hidden = mm_nt(top, order) + mm_nt(rest, order)
    g_gains = jnp.dot(
        jnp.concatenate([g_gain_1, g_gain_2, jnp.zeros((6, width), F32)], axis=0),
        order.astype(F32).T, precision=HIGH,
    )
    g_skip = gate_sums[1].reshape(NH_SSM, HP).sum(axis=1)
    small = jnp.concatenate(
        [g_gains[:2].reshape(-1), g_taps[: KCONV + 1].reshape(-1), gate_sums[0], g_dt_bias, g_a_log, g_skip,
         jnp.zeros((LANES - 3 * NH_SSM,), F32)]
    )
    total = Flow(summing(small.reshape(-1, LANES)))
    grad_hidden = tick([sum_a1, sum_a2, out_1, total], grad_hidden)
    grad_hidden = tick([sum_a1, sum_a2, out_1, total], grad_hidden)
    flows = [sum_a2, total]
    while sum_a2.pending:
        grad_hidden = tick([f for f in (sum_a2, total) if f.pending], grad_hidden)
    out_2 = Flow(completing(jnp.concatenate([sum_a1.value, sum_a2.value], axis=1), 2176))
    while out_2.pending or total.pending:
        grad_hidden = tick([f for f in (out_2, total) if f.pending], grad_hidden)
    early, late = out_1.value, out_2.value
    small = total.value.reshape(-1)
    sizes = [width, width, KCONV * CONV, CONV, INNER, NH_SSM, NH_SSM, NH_SSM]
    starts = [sum(sizes[:k]) for k in range(len(sizes))]
    out_gain_1, out_gain_2, out_conv_w, out_conv_b, out_gain_s, out_dt_bias, out_a_log, out_skip = (
        small[at : at + size] for at, size in zip(starts, sizes)
    )
    return (
        out_hidden,
        grad_hidden,
        out_gain_1,
        late[:, :INNER],
        late[:, conv_at:dt_at],
        late[:, dt_at : dt_at + NH_SSM],
        out_conv_w.reshape(KCONV, CONV),
        out_conv_b,
        out_dt_bias,
        out_a_log,
        out_skip,
        out_gain_s,
        early[:, 3 * hidden : 3 * hidden + INNER].T,
        late[:, q_at:k_at],
        late[:, k_at:v_at],
        late[:, v_at:conv_at],
        early[:, 3 * hidden + INNER :].T,
        out_gain_2,
        early[:, hidden : 2 * hidden],
        early[:, 2 * hidden : 3 * hidden],
        early[:, :hidden].T,
    )


def solution(mesh):
    tokens = P(("rep", "fsdp", "seq"), None)
    wide, tall, same = P(("fsdp", "seq"), None), P(None, ("fsdp", "seq")), P()
    return jax.shard_map(
        body,
        mesh=mesh,
        in_specs=(
            tokens, same, wide, wide, wide, same, same, same, same, same, same, tall,
            wide, wide, wide, tall, same, wide, wide, tall, tokens,
        ),
        out_specs=(
            tokens, tokens, same, wide, wide, wide, same, same, same, same, same, same, tall,
            wide, wide, wide, tall, same, wide, wide, tall,
        ),
        check_vma=False,
    )
```

```python
import functools

import jax
import jax.numpy as jnp
from jax import lax
from jax.experimental import pallas as pl
from jax.experimental.pallas import tpu as pltpu
from jax.sharding import PartitionSpec as P

NH_SSM = 24
HP = 64
NS = 128
KCONV = 4
QUERY_HEADS = 8
KEY_VALUE_HEADS = 2
HEAD_SIZE = 64
BLOCK = 128
INNER = NH_SSM * HP
CONV = INNER + 2 * NS
LANES = 128
PAIRS = NH_SSM // 2

HIGH = lax.Precision.HIGHEST
EPS = 1e-06
ROPE_BASE = 10000.0
SCALE = HEAD_SIZE ** (-0.5)
LOW = jnp.bfloat16
F32 = jnp.float32


def mm(a, b):
    return jnp.dot(a, b, preferred_element_type=F32)


def mm_nt(a, b):
    return lax.dot_general(a, b, (((1,), (1,)), ((), ())), preferred_element_type=F32)


def mm_tn(a, b):
    return lax.dot_general(a, b, (((0,), (0,)), ((), ())), preferred_element_type=F32)


def halves(v):
    top = v.astype(LOW)
    return top, (v - top.astype(F32)).astype(LOW)


def spread(v, heads):
    top, rest = halves(v)
    return mm(top, heads) + mm(rest, heads)


def gather_heads(v, heads):
    top, rest = halves(v)
    return mm_nt(top, heads) + mm_nt(rest, heads)


def lane_halves(shape):
    lane = lax.broadcasted_iota(jnp.int32, shape, len(shape) - 1)
    return lane % LANES < HP


def stacked(pair, left):
    zero = jnp.zeros_like(pair)
    return jnp.concatenate([jnp.where(left, pair, zero), jnp.where(left, zero, pair)], axis=0)


def states_kernel(conv_ref, halo_ref, taps_ref, step_ref, run_ref, heads_ref, pre_ref, end_ref, ext):
    block = pl.program_id(0)

    @pl.when(block == 0)
    def _():
        ext[0:8, :] = halo_ref[...]
        end_ref[...] = jnp.zeros_like(end_ref)

    @pl.when(block > 0)
    def _():
        ext[0:8, :] = ext[BLOCK : BLOCK + 8, :]

    ext[8 : BLOCK + 8, :] = conv_ref[...].astype(F32)
    pre = taps_ref[KCONV : KCONV + 1, :] + jnp.zeros((BLOCK, CONV), F32)
    for j in range(KCONV):
        pre = pre + taps_ref[j : j + 1, :] * ext[5 + j : 5 + j + BLOCK, :]
    pre_ref[...] = pre
    heads = heads_ref[...]
    run = run_ref[...]
    last = run[BLOCK - 1 : BLOCK, :]
    tail = jnp.exp(last - run) * step_ref[...]
    wide = spread(jnp.concatenate([tail, jnp.broadcast_to(jnp.exp(last), (8, LANES))], axis=0), heads)
    inner = pre[:, :INNER]
    x = inner * jax.nn.sigmoid(inner)
    bp = pre[:, INNER : INNER + NS]
    b_low = (bp * jax.nn.sigmoid(bp)).T.astype(LOW)
    weighted = (x * wide[:BLOCK]).astype(LOW)
    end_ref[...] = end_ref[...] * wide[BLOCK : BLOCK + 1] + mm(b_low, weighted)


def mixer_kernel(
    pre_ref, step_ref, run_ref, runt_ref, start_ref, z_ref, gain_ref, skip_ref, heads_ref,
    out_ref, y_ref, sin_ref, sout_ref, state,
):
    block = pl.program_id(0)

    @pl.when(block == 0)
    def _():
        state[...] = start_ref[...]

    heads = heads_ref[...]
    run = run_ref[...]
    runt = runt_ref[...]
    step = step_ref[...]
    pre = pre_ref[...]
    act = pre * jax.nn.sigmoid(pre)
    x = act[:, :INNER]
    b = act[:, INNER : INNER + NS]
    c_low = act[:, INNER + NS :].astype(LOW)
    last = run[BLOCK - 1 : BLOCK, :]
    wide = spread(
        jnp.concatenate(
            [
                step,
                jnp.exp(run),
                jnp.exp(last - run) * step,
                jnp.broadcast_to(jnp.exp(last), (8, LANES)),
            ],
            axis=0,
        ),
        heads,
    )
    x_step = (x * wide[:BLOCK]).astype(LOW)
    old = state[...]
    old_low = old.astype(LOW)
    sin_ref[0] = old_low
    carried = mm(c_low, old_low) * wide[BLOCK : 2 * BLOCK]
    weighted = (x * wide[2 * BLOCK : 3 * BLOCK]).astype(LOW)
    new = old * wide[3 * BLOCK : 3 * BLOCK + 1] + mm(b.T.astype(LOW), weighted)
    state[...] = new
    sout_ref[0] = new.astype(LOW)
    cb = mm_nt(c_low, b.astype(LOW))
    rows = lax.broadcasted_iota(jnp.int32, (BLOCK, BLOCK), 0)
    cols = lax.broadcasted_iota(jnp.int32, (BLOCK, BLOCK), 1)
    causal = rows >= cols
    left = lane_halves((BLOCK, LANES))
    parts = []
    for p in range(PAIRS):
        mixes = []
        for h in (2 * p, 2 * p + 1):
            gap = run[:, h : h + 1] - runt[h : h + 1, :]
            mixes.append((jnp.exp(jnp.where(causal, gap, -1e30)) * cb).astype(LOW))
        pair = x_step[:, p * LANES : (p + 1) * LANES]
        parts.append(mm(jnp.concatenate(mixes, axis=1), stacked(pair, left)))
    y = jnp.concatenate(parts, axis=1) + carried
    y_ref[...] = y
    z = z_ref[...]
    gated = (y + skip_ref[...] * x) * (z * jax.nn.sigmoid(z))
    inv = lax.rsqrt(jnp.mean(gated * gated, axis=-1, keepdims=True) + EPS)
    out_ref[...] = (gated * inv * gain_ref[...]).astype(LOW)


def gate_back_kernel(
    g_ref, y_ref, pre_ref, z_ref, run_ref, gain_ref, skip_ref, heads_ref,
    gy_ref, gz_ref, sums_ref, first_ref,
):
    @pl.when(pl.program_id(0) == 0)
    def _():
        sums_ref[...] = jnp.zeros_like(sums_ref)
        first_ref[...] = jnp.zeros_like(first_ref)

    heads = heads_ref[...]
    run = run_ref[...]
    last = run[BLOCK - 1 : BLOCK, :]
    wide = spread(
        jnp.concatenate([jnp.exp(run), jnp.broadcast_to(jnp.exp(last), (8, LANES))], axis=0), heads
    )
    inner = pre_ref[:, :INNER]
    x = inner * jax.nn.sigmoid(inner)
    cp = pre_ref[:, INNER + NS :]
    c = cp * jax.nn.sigmoid(cp)
    y = y_ref[...] + skip_ref[...] * x
    z = z_ref[...]
    sig = jax.nn.sigmoid(z)
    swish = z * sig
    gated = y * swish
    inv = lax.rsqrt(jnp.mean(gated * gated, axis=-1, keepdims=True) + EPS)
    g = g_ref[...]
    gg = g * gain_ref[...]
    mean = jnp.mean(gg * gated, axis=-1, keepdims=True)
    g_gated = gg * inv - gated * (inv * inv * inv * mean)
    g_y = g_gated * swish
    gz_ref[...] = (g_gated * y * (sig + swish * (1.0 - sig))).astype(LOW)
    gy_ref[...] = g_y.astype(LOW)
    sums_ref[0:1, :] += jnp.sum(g * gated * inv, axis=0, keepdims=True)
    sums_ref[1:2, :] += jnp.sum(g_y * x, axis=0, keepdims=True)
    scaled = (g_y * wide[:BLOCK]).astype(LOW)
    first_ref[...] = first_ref[...] * wide[BLOCK : BLOCK + 1] + mm(c.T.astype(LOW), scaled)


def mixer_back_kernel(
    gy_ref, y_ref, pre_ref, step_ref, run_ref, runt_ref, later_ref, sin_ref, sout_ref,
    conv_ref, before_ref, halo_ref, taps_ref, skip_ref, heads_ref,
    gconv_ref, gtail_ref, rim_ref, gstep_ref, grun_ref, gend_ref, gtaps_ref,
    grad_state, ext, dext,
):
    index = pl.program_id(0)
    count = pl.num_programs(0)

    @pl.when(index == 0)
    def _():
        grad_state[...] = later_ref[...]
        gtaps_ref[...] = jnp.zeros_like(gtaps_ref)
        dext[BLOCK : BLOCK + 8, :] = jnp.zeros((8, CONV), F32)

    @pl.when(index > 0)
    def _():
        dext[BLOCK : BLOCK + 8, :] = dext[0:8, :]

    heads = heads_ref[...]
    run = run_ref[...]
    runt = runt_ref[...]
    step = step_ref[...]
    pre = pre_ref[...]
    sig = jax.nn.sigmoid(pre)
    act = pre * sig
    x = act[:, :INNER]
    b = act[:, INNER : INNER + NS]
    c = act[:, INNER + NS :]
    b_low = b.astype(LOW)
    c_low = c.astype(LOW)
    last = run[BLOCK - 1 : BLOCK, :]
    wide = spread(
        jnp.concatenate(
            [step, jnp.exp(run), jnp.exp(last - run), jnp.broadcast_to(jnp.exp(last), (8, LANES))],
            axis=0,
        ),
        heads,
    )
    step_wide = wide[:BLOCK]
    tail_wide = wide[2 * BLOCK : 3 * BLOCK]
    gy_low = gy_ref[...]
    gy = gy_low.astype(F32)
    x_step = (x * step_wide).astype(LOW)
    later = grad_state[...]
    later_low = later.astype(LOW)
    scaled = (gy * wide[BLOCK : 2 * BLOCK]).astype(LOW)
    weighted = (x * (step_wide * tail_wide)).astype(LOW)
    grad_b = mm_nt(weighted, later_low)
    grad_c = mm_nt(scaled, sin_ref[0])
    from_state = mm(b_low, later_low) * tail_wide
    grad_state[...] = later * wide[3 * BLOCK : 3 * BLOCK + 1] + mm(c.T.astype(LOW), scaled)
    ends = jnp.sum(later * sout_ref[0].astype(F32), axis=0, keepdims=True)
    gend_ref[0] = gather_heads(jnp.broadcast_to(ends, (8, INNER)), heads)
    cbt = mm_nt(b_low, c_low)
    rows = lax.broadcasted_iota(jnp.int32, (BLOCK, BLOCK), 0)
    cols = lax.broadcasted_iota(jnp.int32, (BLOCK, BLOCK), 1)
    left = lane_halves((BLOCK, LANES))
    parts = []
    grad_cb = jnp.zeros((BLOCK, BLOCK), F32)
    for p in range(PAIRS):
        lanes = slice(p * LANES, (p + 1) * LANES)
        gy_stack = stacked(gy_low[:, lanes], left)
        products = mm_nt(gy_stack, x_step[:, lanes])
        mixes = []
        for k, h in enumerate((2 * p, 2 * p + 1)):
            column = jnp.broadcast_to(run[:, h : h + 1], (BLOCK, BLOCK))
            gap = column - runt[h : h + 1, :]
            decay = jnp.exp(jnp.where(rows >= cols, gap, -1e30))
            grad_cb = grad_cb + products[k * BLOCK : (k + 1) * BLOCK] * decay
            decay_t = jnp.exp(jnp.where(cols >= rows, -gap, -1e30))
            mixes.append((decay_t * cbt).astype(LOW))
        parts.append(mm(jnp.concatenate(mixes, axis=1), gy_stack))
    u = jnp.concatenate(parts, axis=1) + from_state
    both = gather_heads(
        jnp.concatenate([gy * y_ref[...], x * u], axis=0), heads
    )
    gstep_ref[...] = both[BLOCK:]
    grun_ref[...] = both[:BLOCK] - step * both[BLOCK:]
    grad_cb_low = grad_cb.astype(LOW)
    grad_c = grad_c + mm(grad_cb_low, b_low)
    grad_b = grad_b + mm(grad_cb.T.astype(LOW), c_low)
    grad_x = u * step_wide + skip_ref[...] * gy
    dpre = jnp.concatenate([grad_x, grad_b, grad_c], axis=1) * (sig + act * (1.0 - sig))
    dext[0:BLOCK, :] = dpre
    k = count - 1 - index
    ext[0:8, :] = jnp.where(k == 0, halo_ref[...], before_ref[BLOCK - 16 :, :].astype(F32)[8:])
    ext[8 : BLOCK + 8, :] = conv_ref[...].astype(F32)
    total = jnp.zeros((BLOCK, CONV), F32)
    for j in range(KCONV):
        total = total + taps_ref[j : j + 1, :] * dext[KCONV - 1 - j : KCONV - 1 - j + BLOCK, :]
        gtaps_ref[j : j + 1, :] += jnp.sum(dpre * ext[5 + j : 5 + j + BLOCK, :], axis=0, keepdims=True)
    gtaps_ref[KCONV : KCONV + 1, :] += jnp.sum(dpre, axis=0, keepdims=True)
    gconv_ref[...] = total.astype(LOW)

    @pl.when(index == 0)
    def _():
        gtail_ref[...] = total[BLOCK - 8 :, :]

    rim_ref[...] = dpre[0:8, :]


def fixed(shape):
    return pl.BlockSpec(shape, lambda i: (0,) * len(shape))


def params(mib):
    return pltpu.CompilerParams(
        dimension_semantics=("arbitrary",), vmem_limit_bytes=mib * 1024 * 1024
    )


def rows_of(width):
    return pl.BlockSpec((BLOCK, width), lambda i: (i, 0))


def mixer_states(conv_low, halo, taps, step, run, heads):
    rows = conv_low.shape[0]
    return pl.pallas_call(
        states_kernel,
        grid=(rows // BLOCK,),
        in_specs=[rows_of(CONV), fixed((8, CONV)), fixed((8, CONV)), rows_of(LANES), rows_of(LANES),
                  fixed((LANES, INNER))],
        out_specs=[rows_of(CONV), fixed((NS, INNER))],
        out_shape=[jax.ShapeDtypeStruct((rows, CONV), F32), jax.ShapeDtypeStruct((NS, INNER), F32)],
        scratch_shapes=[pltpu.VMEM((BLOCK + 8, CONV), F32)],
        compiler_params=params(14),
        name="mixer_states",
    )(conv_low, halo, taps, step, run, heads)


def mixer_forward(pre, step, run, runt, start, z, gain, skip, heads):
    rows = pre.shape[0]
    count = rows // BLOCK
    state_spec = pl.BlockSpec((1, NS, INNER), lambda i: (i, 0, 0))
    return pl.pallas_call(
        mixer_kernel,
        grid=(count,),
        in_specs=[rows_of(CONV), rows_of(LANES), rows_of(LANES), rows_of(LANES), fixed((NS, INNER)),
                  rows_of(INNER), fixed((1, INNER)), fixed((1, INNER)), fixed((LANES, INNER))],
        out_specs=[rows_of(INNER), rows_of(INNER), state_spec, state_spec],
        out_shape=[
            jax.ShapeDtypeStruct((rows, INNER), LOW),
            jax.ShapeDtypeStruct((rows, INNER), F32),
            jax.ShapeDtypeStruct((count, NS, INNER), LOW),
            jax.ShapeDtypeStruct((count, NS, INNER), LOW),
        ],
        scratch_shapes=[pltpu.VMEM((NS, INNER), F32)],
        compiler_params=params(14),
        name="mixer_forward",
    )(pre, step, run, runt, start, z, gain, skip, heads)


def gate_back(g, y, pre, z, run, gain, skip, heads):
    rows = pre.shape[0]
    count = rows // BLOCK

    def back(width):
        return pl.BlockSpec((BLOCK, width), lambda i: (count - 1 - i, 0))

    return pl.pallas_call(
        gate_back_kernel,
        grid=(count,),
        in_specs=[back(INNER), back(INNER), back(CONV), back(INNER), back(LANES), fixed((1, INNER)),
                  fixed((1, INNER)), fixed((LANES, INNER))],
        out_specs=[back(INNER), back(INNER), fixed((8, INNER)), fixed((NS, INNER))],
        out_shape=[
            jax.ShapeDtypeStruct((rows, INNER), LOW),
            jax.ShapeDtypeStruct((rows, INNER), LOW),
            jax.ShapeDtypeStruct((8, INNER), F32),
            jax.ShapeDtypeStruct((NS, INNER), F32),
        ],
        compiler_params=params(14),
        name="gate_back",
    )(g, y, pre, z, run, gain, skip, heads)


def mixer_back(gy, y, pre, step, run, runt, later, s_in, s_out, conv_low, halo, taps, skip, heads):
    rows = pre.shape[0]
    count = rows // BLOCK

    def back(width):
        return pl.BlockSpec((BLOCK, width), lambda i: (count - 1 - i, 0))

    state_spec = pl.BlockSpec((1, NS, INNER), lambda i: (count - 1 - i, 0, 0))
    before = pl.BlockSpec((BLOCK, CONV), lambda i: (jnp.maximum(count - 2 - i, 0), 0))
    return pl.pallas_call(
        mixer_back_kernel,
        grid=(count,),
        in_specs=[back(INNER), back(INNER), back(CONV), back(LANES), back(LANES), back(LANES),
                  fixed((NS, INNER)), state_spec, state_spec, back(CONV), before, fixed((8, CONV)),
                  fixed((8, CONV)), fixed((1, INNER)), fixed((LANES, INNER))],
        out_specs=[back(CONV), fixed((8, CONV)), fixed((8, CONV)), back(LANES), back(LANES),
                   pl.BlockSpec((1, 8, LANES), lambda i: (count - 1 - i, 0, 0)), fixed((8, CONV))],
        out_shape=[
            jax.ShapeDtypeStruct((rows, CONV), LOW),
            jax.ShapeDtypeStruct((8, CONV), F32),
            jax.ShapeDtypeStruct((8, CONV), F32),
            jax.ShapeDtypeStruct((rows, LANES), F32),
            jax.ShapeDtypeStruct((rows, LANES), F32),
            jax.ShapeDtypeStruct((count, 8, LANES), F32),
            jax.ShapeDtypeStruct((8, CONV), F32),
        ],
        scratch_shapes=[
            pltpu.VMEM((NS, INNER), F32),
            pltpu.VMEM((BLOCK + 8, CONV), F32),
            pltpu.VMEM((BLOCK + 8, CONV), F32),
        ],
        compiler_params=params(22),
        name="mixer_back",
    )(gy, y, pre, step, run, runt, later, s_in, s_out, conv_low, conv_low, halo, taps, skip, heads)


def turned(x, cosine, sine):
    half = HEAD_SIZE // 2
    lane = lax.broadcasted_iota(jnp.int32, x.shape, 1)
    other = jnp.where(
        lane % HEAD_SIZE < half, pltpu.roll(x, LANES - half, axis=1), pltpu.roll(x, half, axis=1)
    )
    return x * cosine + other * sine


def group_keys(value, group, left):
    other = pltpu.roll(value, HEAD_SIZE, axis=1)
    return jnp.where(left == (group == 0), value, other).astype(LOW)


def group_rows(value, group):
    turned_over = value.T
    return jnp.where(group == 0, turned_over[:HEAD_SIZE], turned_over[HEAD_SIZE:]).astype(LOW)


def attend_kernel(first_ref, q_ref, cos_ref, sin_ref, kv_ref, out_ref, q_low_ref, norm_ref):
    keys, rows = kv_ref.shape[0], q_ref.shape[0]
    group = pl.program_id(0) // 2
    left = lane_halves((rows, LANES))
    key_at = lax.broadcasted_iota(jnp.int32, (keys, rows), 0)
    query_at = lax.broadcasted_iota(jnp.int32, (keys, rows), 1) + first_ref[0]
    seen = key_at <= query_at
    q = (turned(q_ref[...], cos_ref[...], sin_ref[...]).astype(LOW) * SCALE).astype(LOW)
    q_low_ref[...] = q
    k = group_keys(kv_ref[:, :LANES].astype(F32), group, lane_halves((keys, LANES)))
    vt = group_rows(kv_ref[:, LANES:].astype(F32), group)
    zero = jnp.zeros_like(q)
    parts = []
    norm_ref[...] = jnp.zeros_like(norm_ref)
    for n in range(2):
        mine = jnp.where(left, q, zero) if n == 0 else jnp.where(left, zero, q)
        scores = jnp.where(seen, mm_nt(k, mine), -1e30)
        peak = jnp.max(scores, axis=0, keepdims=True)
        raised = jnp.exp(scores - peak)
        total = jnp.sum(raised, axis=0, keepdims=True)
        probs = (raised * (1.0 / total)).astype(LOW)
        norm_ref[0, n : n + 1, :] = peak + jnp.log(total)
        parts.append(mm(vt, probs))
    out_ref[...] = jnp.concatenate(parts, axis=0).T.astype(LOW)


def attend_back_kernel(
    first_ref, g_ref, q_ref, cos_ref, sin_ref, kv_ref, norm_ref, gq_ref, gkv_ref
):
    keys, rows = kv_ref.shape[0], q_ref.shape[0]
    step = pl.program_id(0)
    group = step // 2
    left = lane_halves((rows, LANES))
    key_left = lane_halves((keys, LANES))
    key_at = lax.broadcasted_iota(jnp.int32, (keys, rows), 0)
    query_at = lax.broadcasted_iota(jnp.int32, (keys, rows), 1) + first_ref[0]
    seen = key_at <= query_at
    q = q_ref[...]
    g = g_ref[...].astype(LOW)
    k_wide = kv_ref[:, :LANES].astype(F32)
    k = group_keys(k_wide, group, key_left)
    kt = group_rows(k_wide, group)
    v = group_keys(kv_ref[:, LANES:].astype(F32), group, key_left)
    zero = jnp.zeros_like(q)
    parts = []
    gk = jnp.zeros((keys, LANES), F32)
    gv = jnp.zeros((keys, LANES), F32)
    for n in range(2):
        mine = jnp.where(left, q, zero) if n == 0 else jnp.where(left, zero, q)
        grad = jnp.where(left, g, zero) if n == 0 else jnp.where(left, zero, g)
        scores = jnp.where(seen, mm_nt(k, mine), -1e30)
        probs = jnp.exp(scores - norm_ref[0, n : n + 1, :])
        g_probs = mm_nt(v, grad)
        inner = jnp.sum(probs * g_probs, axis=0, keepdims=True)
        g_scores = (probs * (g_probs - inner)).astype(LOW)
        gk = gk + mm(g_scores, mine)
        gv = gv + mm(probs.astype(LOW), grad)
        parts.append(mm(kt, g_scores))
    grad_q = jnp.concatenate(parts, axis=0).T * SCALE
    gq_ref[...] = turned(grad_q, cos_ref[...], -sin_ref[...]).astype(LOW)
    here = key_left == (group == 0)

    @pl.when(step == 0)
    def _():
        gkv_ref[...] = jnp.zeros_like(gkv_ref)

    for n, value in enumerate((gk, gv)):
        both = value + pltpu.roll(value, HEAD_SIZE, axis=1)
        gkv_ref[:, n * LANES : (n + 1) * LANES] += jnp.where(here, both, 0.0)


def attend(first, proj, q_at, cosine, sine, kv):
    rows, keys = proj.shape[0], kv.shape[0]
    count = QUERY_HEADS // 2
    column = pl.BlockSpec((rows, LANES), lambda i: (0, i))
    low = jax.ShapeDtypeStruct((rows, QUERY_HEADS * HEAD_SIZE), LOW)
    return pl.pallas_call(
        attend_kernel,
        grid=(count,),
        in_specs=[
            pl.BlockSpec(memory_space=pltpu.SMEM),
            pl.BlockSpec((rows, LANES), lambda i: (0, q_at // LANES + i)),
            fixed((rows, LANES)),
            fixed((rows, LANES)),
            fixed((keys, 2 * LANES)),
        ],
        out_specs=[column, column, pl.BlockSpec((1, 8, rows), lambda i: (i, 0, 0))],
        out_shape=[low, low, jax.ShapeDtypeStruct((count, 8, rows), F32)],
        compiler_params=params(22),
        name="attend",
    )(first, proj, cosine, sine, kv)


def attend_back(first, g, g_at, q, cosine, sine, kv, norm):
    rows, keys = q.shape[0], kv.shape[0]
    count = QUERY_HEADS // 2
    column = pl.BlockSpec((rows, LANES), lambda i: (0, i))
    return pl.pallas_call(
        attend_back_kernel,
        grid=(count,),
        in_specs=[
            pl.BlockSpec(memory_space=pltpu.SMEM),
            pl.BlockSpec((rows, LANES), lambda i: (0, g_at // LANES + i)),
            column,
            fixed((rows, LANES)),
            fixed((rows, LANES)),
            fixed((keys, 2 * LANES)),
            pl.BlockSpec((1, 8, rows), lambda i: (i, 0, 0)),
        ],
        out_specs=[column, fixed((keys, 2 * LANES))],
        out_shape=[
            jax.ShapeDtypeStruct(q.shape, LOW),
            jax.ShapeDtypeStruct((keys, 2 * LANES), F32),
        ],
        compiler_params=params(22),
        name="attend_back",
    )(first, g, q, cosine, sine, kv, norm)


def trade(value, axis, bit):
    count = lax.axis_size(axis)
    return lax.ppermute(value, axis, [(i, i ^ bit) for i in range(count)])


def shifted(value, axis, by):
    count = lax.axis_size(axis)
    return lax.ppermute(value, axis, [(i, (i + by) % count) for i in range(count)])


def from_behind(value, axis, by):
    count = lax.axis_size(axis)
    pairs = [(i, i + by) for i in range(count) if 0 <= i + by < count]
    return lax.ppermute(value, axis, pairs)


def bits_of(count, flip):
    bits = [1 << k for k in range(count.bit_length() - 1)]
    return bits[::-1] if flip else bits


class Flow:
    def __init__(self, steps):
        self.steps, self.value = steps, None
        self.pending = next(steps)

    def advance(self, arrived):
        try:
            self.pending = self.steps.send(arrived)
        except StopIteration as end:
            self.pending, self.value = [], end.value


def tick(flows, values):
    flows = [f for f in flows if f.pending]
    arrived, values = lax.optimization_barrier(([f.pending for f in flows], values))
    for flow, got in zip(flows, arrived):
        flow.advance(got)
    return values


def result(flow):
    while flow.pending:
        tick([flow], ())
    return flow.value


def sharing(own, split):
    reps = lax.axis_size("rep")
    held = [{0: own[:, :split]}, {0: own[:, split:]}]
    for bits in zip(bits_of(reps, False), bits_of(reps, True)):
        orders = [sorted(h) for h in held]
        sent = [jnp.concatenate([h[b] for b in order], axis=0) for h, order in zip(held, orders)]
        got = yield [trade(v, "rep", bit) for v, bit in zip(sent, bits)]
        for h, order, bit, value in zip(held, orders, bits, got):
            value = value.reshape(len(order), -1, value.shape[1])
            for k, b in enumerate(order):
                h[b ^ bit] = value[k]
    return [[h[b] for b in range(reps)] for h in held]


def gathering(shard, split):
    reps, depth = lax.axis_size("rep"), lax.axis_size("fsdp")
    rep = lax.axis_index("rep")
    unit = shard.shape[0] // reps
    quarters = [lax.dynamic_slice_in_dim(shard, (rep ^ b) * unit, unit, 0) for b in range(reps)]
    near = {0: quarters[0]}
    for bit in bits_of(depth, True):
        order = sorted(near)
        (got,) = yield [trade(jnp.concatenate([near[s] for s in order], axis=0), "fsdp", bit)]
        for k, s in enumerate(order):
            near[s ^ bit] = got[k * unit : (k + 1) * unit]
    shared = yield from sharing(jnp.concatenate([near[s] for s in range(1, depth)], axis=0), split)
    sides = []
    for side, columns in zip(shared, (slice(0, split), slice(split, None))):
        parts = [part for b in range(reps) for part in (quarters[b][:, columns], side[b])]
        sides.append(jnp.concatenate(parts, axis=0))
    own = jnp.concatenate(sides, axis=1)
    return [own] + (yield [trade(own, "seq", a) for a in range(1, lax.axis_size("seq"))])


def reducing(left, right, split):
    seqs, reps, depth = lax.axis_size("seq"), lax.axis_size("rep"), lax.axis_size("fsdp")
    part = left.shape[1] // seqs
    sent = [mm_tn(left[:, a * part : (a + 1) * part], right).astype(LOW) for a in range(1, seqs)]
    got = yield [trade(value, "seq", a + 1) for a, value in enumerate(sent)]
    total = mm_tn(left[:, :part], right)
    for value in got:
        total = total + value.astype(F32)
    total = total.reshape(reps, part // reps, right.shape[1])
    held = [{b: total[b, :, :split] for b in range(reps)}, {b: total[b, :, split:] for b in range(reps)}]
    for bits in zip(bits_of(reps, False), bits_of(reps, True)):
        away = [sorted(b for b in h if b & bit) for h, bit in zip(held, bits)]
        sent = [jnp.concatenate([h[b] for b in bs], axis=0).astype(LOW) for h, bs in zip(held, away)]
        got = yield [trade(v, "rep", bit) for v, bit in zip(sent, bits)]
        for n, (h, bs, bit, value) in enumerate(zip(held, away, bits, got)):
            value = value.reshape(len(bs), -1, value.shape[1])
            held[n] = {b: h[b] + value[bs.index(b ^ bit)].astype(F32) for b in h if not b & bit}
    mine = jnp.concatenate([held[0][0], held[1][0]], axis=1).reshape(depth, -1, right.shape[1])
    near = {s: mine[s] for s in range(depth)}
    for bit in bits_of(depth, False):
        away = [s for s in sorted(near) if s & bit]
        (got,) = yield [trade(jnp.stack([near[s] for s in away]).astype(LOW), "fsdp", bit)]
        near = {s: near[s] + got[away.index(s ^ bit)].astype(F32) for s in near if not s & bit}
    return near[0].astype(LOW)


def completing(own, split):
    left, right = yield from sharing(own, split)
    rep = lax.axis_index("rep")
    sides = []
    for side in (left, right):
        stack = jnp.stack(side)
        ordered = [lax.dynamic_index_in_dim(stack, rep ^ q, 0, False) for q in range(len(side))]
        sides.append(jnp.concatenate(ordered, axis=0))
    return jnp.concatenate(sides, axis=1).astype(F32)


def summing(value):
    for axis in ("seq", "rep", "fsdp"):
        count = lax.axis_size(axis)
        place = lax.axis_index(axis)
        got = yield [trade(value, axis, other) for other in range(1, count)]
        held = jnp.stack([value] + got)
        value = sum(lax.dynamic_index_in_dim(held, place ^ k, 0, False) for k in range(count))
    return value


def copied(name, scalars, arrays, outs, plan):
    def kernel(*refs):
        numbers, refs = refs[: len(scalars)], refs[len(scalars) :]
        sources, targets = refs[: len(arrays)], refs[len(arrays) :]
        for a, at, o, to in plan(numbers):
            targets[o][to] = sources[a][at]

    whole = pl.BlockSpec(memory_space=pltpu.VMEM)
    return pl.pallas_call(
        kernel,
        in_specs=[pl.BlockSpec(memory_space=pltpu.SMEM)] * len(scalars) + [whole] * len(arrays),
        out_specs=[whole] * len(outs),
        out_shape=[jax.ShapeDtypeStruct(shape, LOW) for shape in outs],
        compiler_params=pltpu.CompilerParams(vmem_limit_bytes=16 * 1024 * 1024),
        name=name,
    )(*scalars, *arrays)


def span(start, size):
    return slice(start, start + size)


def quarter(rep, b, unit):
    return pl.ds(pl.multiple_of((rep[0] ^ b) * unit, unit), unit)


def gathering_fast(shards, split):
    reps, depth = lax.axis_size("rep"), lax.axis_size("fsdp")
    rep = lax.axis_index("rep").astype(jnp.int32)[None]
    unit = shards[0].shape[0] // reps
    sizes = [w.shape[1] for w in shards]
    places = [sum(sizes[:k]) for k in range(len(sizes))]
    width, every = sum(sizes), slice(None)
    (mine,) = copied(
        "pick", [rep], shards, [(unit, width)],
        lambda n: [(k, (quarter(n[0], 0, unit), every), 0, (every, span(at, size)))
                   for k, (at, size) in enumerate(zip(places, sizes))],
    )
    (second,) = yield [trade(mine, "fsdp", 2)]
    (pair,) = copied(
        "pair", [], [mine, second], [(2 * unit, width)],
        lambda n: [(k, (every, every), 0, (span(k * unit, unit), every)) for k in range(2)],
    )
    (others,) = yield [trade(pair, "fsdp", 1)]
    rows = (depth - 1) * unit
    columns = (span(0, split), span(split, width - split))
    narrow = (split, width - split)
    first = copied(
        "split", [], [others, second], [(rows, n) for n in narrow],
        lambda n: [(k, (span(at * unit, unit), columns[o]), o, (span(s * unit, unit), every))
                   for s, (k, at) in enumerate([(0, 0), (1, 0), (0, 1)]) for o in range(2)],
    )
    one = yield [trade(first[0], "rep", 1), trade(first[1], "rep", 2)]
    joined = copied(
        "join", [], [first[0], one[0], first[1], one[1]], [(2 * rows, n) for n in narrow],
        lambda n: [(2 * o + k, (every, every), o, (span(k * rows, rows), every)) for o in range(2) for k in range(2)],
    )
    two = yield [trade(joined[0], "rep", 2), trade(joined[1], "rep", 1)]
    tall = reps * depth * unit
    pieces = [first[0], one[0], two[0], first[1], one[1], two[1]]
    found = [(0, 0, 0, 0), (1, 0, 1, 0), (2, 0, 2, 0), (2, 1, 3, 0), (3, 0, 0, 1), (4, 0, 2, 1), (5, 0, 1, 1), (5, 1, 3, 1)]

    def plan(n):
        moves = []
        for b in range(reps):
            for k, (at, size) in enumerate(zip(places, sizes)):
                moves.append((k, (quarter(n[0], b, unit), every), 0, (span(b * depth * unit, unit), span(at, size))))
        for piece, part, b, o in found:
            moves.append((len(shards) + piece, (span(part * rows, rows), every), 0,
                          (span(b * depth * unit + unit, rows), columns[o])))
        return moves

    (own,) = copied("assemble", [rep], list(shards) + pieces, [(tall, width)], plan)
    return [own] + (yield [trade(own, "seq", a) for a in range(1, lax.axis_size("seq"))])


def product(left, which, right, tile):
    if right.ndim == 2:
        right = right[None]
    tokens, width = left.shape[0], right.shape[0] * right.shape[2]
    per = right.shape[2] // tile
    part = left.shape[1] // lax.axis_size("seq")

    def kernel(left_ref, right_ref, out_ref, turned_left):
        @pl.when(pl.program_id(0) == 0)
        def _():
            turned_left[...] = left_ref[...].astype(F32).T.astype(LOW)

        out_ref[...] = mm(turned_left[...], right_ref[0]).astype(LOW)

    return pl.pallas_call(
        kernel,
        grid=(width // tile,),
        in_specs=[pl.BlockSpec((tokens, part), lambda i: (0, which)),
                  pl.BlockSpec((1, tokens, tile), lambda i: (i // per, 0, i % per))],
        out_specs=pl.BlockSpec((part, tile), lambda i: (0, i)),
        out_shape=jax.ShapeDtypeStruct((part, width), LOW),
        scratch_shapes=[pltpu.VMEM((part, tokens), LOW)],
        compiler_params=params(14),
        name="product",
    )(left, right)


def product_parts(left, right, got, split, tile):
    if right.ndim == 2:
        right = right[None]
    tokens, width = left.shape[0], right.shape[0] * right.shape[2]
    per = right.shape[2] // tile
    part = left.shape[1] // lax.axis_size("seq")
    rows = part // 4
    low_tiles = split // tile

    def kernel(left_ref, right_ref, got_ref, sent_l, kept_l, sent_r, kept_r, turned_left):
        i = pl.program_id(0)

        @pl.when(i == 0)
        def _():
            turned_left[...] = left_ref[...].astype(F32).T.astype(LOW)

        total = mm(turned_left[...], right_ref[0]) + got_ref[...].astype(F32)
        b = [total[k * rows : (k + 1) * rows] for k in range(4)]

        @pl.when(i < low_tiles)
        def _():
            sent_l[0], sent_l[1] = b[1].astype(LOW), b[3].astype(LOW)
            kept_l[0], kept_l[1] = b[0], b[2]

        @pl.when(i >= low_tiles)
        def _():
            sent_r[0], sent_r[1] = b[2].astype(LOW), b[3].astype(LOW)
            kept_r[0], kept_r[1] = b[0], b[1]

    def left_spec():
        return pl.BlockSpec((2, rows, tile), lambda i: (0, 0, jnp.minimum(i, low_tiles - 1)))

    def right_spec():
        return pl.BlockSpec((2, rows, tile), lambda i: (0, 0, jnp.maximum(i - low_tiles, 0)))

    def shape(n, kind):
        return jax.ShapeDtypeStruct((2, rows, n), kind)

    return pl.pallas_call(
        kernel,
        grid=(width // tile,),
        in_specs=[pl.BlockSpec((tokens, part), lambda i: (0, 0)),
                  pl.BlockSpec((1, tokens, tile), lambda i: (i // per, 0, i % per)),
                  pl.BlockSpec((part, tile), lambda i: (0, i))],
        out_specs=[left_spec(), left_spec(), right_spec(), right_spec()],
        out_shape=[shape(split, LOW), shape(split, F32), shape(width - split, LOW), shape(width - split, F32)],
        scratch_shapes=[pltpu.VMEM((part, tokens), LOW)],
        compiler_params=params(14),
        name="product_parts",
    )(left, right, got)


def folded(kept, got):
    rows, step = kept[0].shape[1], 32

    def kernel(kl, gl, kr, gr, sl, ol, sr, o_r):
        for k, g, sent, own in ((kl, gl, sl, ol), (kr, gr, sr, o_r)):
            own[...] = k[0] + g[0].astype(F32)
            sent[...] = (k[1] + g[1].astype(F32)).astype(LOW)

    def thick(n):
        return pl.BlockSpec((2, step, n), lambda i: (0, i, 0))

    def flat(n):
        return pl.BlockSpec((step, n), lambda i: (i, 0))

    a, b = kept[0].shape[2], kept[1].shape[2]
    return pl.pallas_call(
        kernel,
        grid=(rows // step,),
        in_specs=[thick(a), thick(a), thick(b), thick(b)],
        out_specs=[flat(a), flat(a), flat(b), flat(b)],
        out_shape=[jax.ShapeDtypeStruct((rows, n), kind) for n in (a, b) for kind in (LOW, F32)],
        compiler_params=params(14),
        name="folded",
    )(kept[0], got[0], kept[1], got[1])


def spread_depth(kept, got):
    rows, a = kept[0].shape
    unit, width = rows // 4, a + kept[1].shape[1]

    def kernel(kl, gl, kr, gr, own, sent):
        for k, g, columns in ((kl, gl, slice(0, a)), (kr, gr, slice(a, width))):
            total = k[...] + g[...].astype(F32)
            for s in range(4):
                piece, at = total[s * unit : (s + 1) * unit], slice(s // 2 * unit, (s // 2 + 1) * unit)
                if s % 2:
                    sent[at, columns] = piece.astype(LOW)
                else:
                    own[at, columns] = piece

    return pl.pallas_call(
        kernel,
        out_shape=[jax.ShapeDtypeStruct((2 * unit, width), F32), jax.ShapeDtypeStruct((2 * unit, width), LOW)],
        compiler_params=pltpu.CompilerParams(vmem_limit_bytes=16 * 1024 * 1024),
        name="spread_depth",
    )(kept[0], got[0], kept[1], got[1])


def last_fold(kept, got):
    rows, width = kept.shape
    unit = rows // 2

    def kernel(k, g, own, sent):
        own[...] = k[:unit] + g[:unit].astype(F32)
        sent[...] = (k[unit:] + g[unit:].astype(F32)).astype(LOW)

    return pl.pallas_call(
        kernel,
        out_shape=[jax.ShapeDtypeStruct((unit, width), F32), jax.ShapeDtypeStruct((unit, width), LOW)],
        compiler_params=pltpu.CompilerParams(vmem_limit_bytes=16 * 1024 * 1024),
        name="last_fold",
    )(kept, got)


def reducing_fast(left, right, split, tile):
    seqs = lax.axis_size("seq")
    wide = right.shape[-1]
    wide = next(n for n in (1152, 1024, 768, 512, 384, 128) if wide % n == 0)
    sent = [product(left, a, right, wide) for a in range(1, seqs)]
    got = yield [trade(value, "seq", a + 1) for a, value in enumerate(sent)]
    got = got[0] if seqs == 2 else sum(v.astype(F32) for v in got)
    sent_l, kept_l, sent_r, kept_r = product_parts(left, right, got, split, tile)
    got = yield [trade(sent_l, "rep", 1), trade(sent_r, "rep", 2)]
    sent_l, kept_l, sent_r, kept_r = folded((kept_l, kept_r), got)
    got = yield [trade(sent_l, "rep", 2), trade(sent_r, "rep", 1)]
    own, sent = spread_depth((kept_l, kept_r), got)
    (got,) = yield [trade(sent, "fsdp", 1)]
    own, sent = last_fold(own, got)
    (got,) = yield [trade(sent, "fsdp", 2)]
    return (own + got.astype(F32)).astype(LOW)


def finishing(own, split, layout):
    reps = lax.axis_size("rep")
    unit, width = own.shape
    sides = (own[:, :split], own[:, split:])
    one = yield [trade(sides[0], "rep", 1), trade(sides[1], "rep", 2)]
    two = yield [trade(jnp.concatenate([sides[0], one[0]], axis=0), "rep", 2),
                 trade(jnp.concatenate([sides[1], one[1]], axis=0), "rep", 1)]
    rep = lax.axis_index("rep").astype(jnp.int32)[None]

    def kernel(rep_ref, own_ref, l1, r1, l2, r2, *outs):
        r = rep_ref[0]
        sections = (
            (0, split, (own_ref[:, :split], l1[...], l2[:unit], l2[unit:])),
            (split, width - split, (own_ref[:, split:], r2[:unit], r1[...], r2[unit:])),
        )
        for (first, count, flip), out in zip(layout, outs):
            for start, size, parts in sections:
                low, high = max(first, start), min(first + count, start + size)
                if low >= high:
                    continue
                parts = [p[:, low - start : min(-(-(high - start) // LANES) * LANES, size)].astype(F32) for p in parts]
                rows = []
                for q in range(reps):
                    chosen = parts[0]
                    for b in range(1, reps):
                        chosen = jnp.where((r ^ q) == b, parts[b], chosen)
                    rows.append(chosen)
                block = jnp.concatenate(rows, axis=0)
                if flip:
                    out[low - first : high - first, :] = block.T
                else:
                    out[:, low - first : high - first] = block[:, : high - low]

    whole = pl.BlockSpec(memory_space=pltpu.VMEM)
    return pl.pallas_call(
        kernel,
        in_specs=[pl.BlockSpec(memory_space=pltpu.SMEM)] + [whole] * 5,
        out_specs=[whole] * len(layout),
        out_shape=[
            jax.ShapeDtypeStruct((count, reps * unit) if flip else (reps * unit, count), F32)
            for _, count, flip in layout
        ],
        compiler_params=pltpu.CompilerParams(vmem_limit_bytes=16 * 1024 * 1024),
        name="finishing",
    )(rep, own, one[0], one[1], two[0], two[1])


def gather_flow(shards, split):
    unit = shards[0].shape[0] // lax.axis_size("rep")
    if unit % 16 == 0 and lax.axis_size("rep") == 4 and lax.axis_size("fsdp") == 4:
        return Flow(gathering_fast(shards, split))
    return Flow(gathering(jnp.concatenate(shards, axis=1), split))


def reduce_flow(left, right, split, tile):
    unit = left.shape[1] // (lax.axis_size("rep") * lax.axis_size("fsdp") * lax.axis_size("seq"))
    if unit % 16 == 0 and lax.axis_size("rep") == 4 and lax.axis_size("fsdp") == 4:
        return Flow(reducing_fast(left, right, split, tile))
    if right.ndim == 3:
        right = jnp.concatenate(list(right), axis=1)
    return Flow(reducing(left, right, split))


def finish_flow(own, split, layout):
    def plain():
        total = yield from completing(own, split)
        pieces = [total[:, first : first + count] for first, count, _ in layout]
        return [piece.T if flip else piece for piece, (_, _, flip) in zip(pieces, layout)]

    if own.shape[0] % 16 == 0 and lax.axis_size("rep") == 4:
        return Flow(finishing(own, split, layout))
    return Flow(plain())


def summed(x, weights, part):
    return sum(mm(x[:, a * part : (a + 1) * part], w[...]) for a, w in enumerate(weights))


def project(x, weight, tile):
    rows, width, part = x.shape[0], weight[0].shape[1], weight[0].shape[0]

    def kernel(x_ref, *refs):
        refs[-1][...] = summed(x_ref, refs[:-1], part)

    return pl.pallas_call(
        kernel,
        grid=(width // tile,),
        in_specs=[fixed(x.shape)] + [pl.BlockSpec((part, tile), lambda i: (0, i))] * len(weight),
        out_specs=pl.BlockSpec((rows, tile), lambda i: (0, i)),
        out_shape=jax.ShapeDtypeStruct((rows, width), F32),
        compiler_params=params(14),
        name="project",
    )(x, *weight)


def feed_forward(x, weight, tile):
    rows, width, part = x.shape[0], weight[0].shape[1] // 2, weight[0].shape[0]
    count, steps = len(weight), width // tile

    def kernel(x_ref, *refs):
        gate = summed(x_ref, refs[:count], part)
        up = summed(x_ref, refs[count : 2 * count], part)
        gate_ref, up_ref, act_ref = refs[2 * count :]
        gate_ref[...] = gate.astype(LOW)
        up_ref[...] = up.astype(LOW)
        act_ref[...] = (gate * jax.nn.sigmoid(gate) * up).astype(LOW)

    column = pl.BlockSpec((rows, tile), lambda i: (0, i))
    return pl.pallas_call(
        kernel,
        grid=(steps,),
        in_specs=[fixed(x.shape)] + [pl.BlockSpec((part, tile), lambda i: (0, i))] * count
        + [pl.BlockSpec((part, tile), lambda i: (0, steps + i))] * count,
        out_specs=[column] * 3,
        out_shape=[jax.ShapeDtypeStruct((rows, width), LOW)] * 3,
        compiler_params=params(14),
        name="feed_forward",
    )(x, *weight, *weight)


def feed_back(g, weight, gate, up, tile):
    rows, width, part = g.shape[0], weight[0].shape[1], weight[0].shape[0]

    def kernel(g_ref, gate_ref, up_ref, *refs):
        grad = summed(g_ref, refs[:-1], part)
        value = gate_ref[...].astype(F32)
        sig = jax.nn.sigmoid(value)
        swish = value * sig
        refs[-1][0] = (grad * up_ref[...].astype(F32) * (sig + swish * (1.0 - sig))).astype(LOW)
        refs[-1][1] = (grad * swish).astype(LOW)

    column = pl.BlockSpec((rows, tile), lambda i: (0, i))
    return pl.pallas_call(
        kernel,
        grid=(width // tile,),
        in_specs=[fixed(g.shape), column, column] + [pl.BlockSpec((part, tile), lambda i: (0, i))] * len(weight),
        out_specs=pl.BlockSpec((2, rows, tile), lambda i: (0, 0, i)),
        out_shape=jax.ShapeDtypeStruct((2, rows, width), LOW),
        compiler_params=params(14),
        name="feed_back",
    )(g, gate, up, *weight)


def into(x, weight):
    part = x.shape[1] // len(weight)
    return sum(mm(x[:, a * part : (a + 1) * part], w) for a, w in enumerate(weight))


def out_of(pairs):
    count = len(pairs[0][1])
    return jnp.concatenate([sum(mm_nt(g, weight[a]) for g, weight in pairs) for a in range(count)], axis=1)


def rms_back(g, v, gain):
    r = lax.rsqrt(jnp.mean(v * v, axis=-1, keepdims=True) + EPS)
    scaled = g * gain
    mean = jnp.mean(scaled * v, axis=-1, keepdims=True)
    return r * scaled - v * (r * r * r * mean), jnp.sum(g * v * r, axis=0, keepdims=True)


def rms_gain(v, gain):
    return v * lax.rsqrt(jnp.mean(v * v, axis=-1, keepdims=True) + EPS) * gain


def swap_halves(x):
    half = HEAD_SIZE // 2
    pieces = []
    for start in range(0, x.shape[1], HEAD_SIZE):
        pieces += [x[:, start + half : start + HEAD_SIZE], x[:, start : start + half]]
    return jnp.concatenate(pieces, axis=1)


def body(
    hidden_in, norm1_gain, w_z, w_xbc, w_dt, conv_w, conv_b, dt_bias, a_log, d_skip, ssm_gain, w_ssm_out,
    w_q, key_weight, value_weight, w_o, norm2_gain, w_gate, w_up, w_down, grad_out,
):
    rows, width = hidden_in.shape
    seqs, reps, depth = lax.axis_size("seq"), lax.axis_size("rep"), lax.axis_size("fsdp")
    core, rep, deep = lax.axis_index("seq"), lax.axis_index("rep"), lax.axis_index("fsdp")
    shard = w_z.shape[0]
    unit = shard // reps
    blocks = rows // BLOCK

    place = jnp.arange(width, dtype=jnp.int32)
    u, s = place % unit, place // unit % depth
    b, a = place // (unit * depth) % reps, place // (unit * depth * reps)
    source = (((deep ^ s) * seqs + (core ^ a)) * reps + (rep ^ b)) * unit + u
    order = (place[:, None] == source[None, :]).astype(LOW)

    pack_a = [w_z, w_xbc, jnp.pad(w_dt, ((0, 0), (0, LANES - NH_SSM))), w_q, key_weight, value_weight]
    conv_at, dt_at, q_at = INNER, INNER + CONV, INNER + CONV + LANES
    k_at, v_at = q_at + 512, q_at + 640
    flow_a = gather_flow(pack_a, 2176)
    pack_b = jnp.concatenate([w_ssm_out, w_o], axis=0).T
    pack_c = [w_gate, w_up]
    pack_d = w_down.T
    gains = jnp.dot(
        jnp.concatenate([norm1_gain[None], norm2_gain[None], jnp.zeros((6, width), F32)], axis=0),
        order.astype(F32), precision=HIGH,
    )
    gain_1, gain_2 = gains[0:1], gains[1:2]
    inputs = mm(hidden_in, order)
    normed_1 = rms_gain(inputs, gain_1).astype(LOW)
    inputs = inputs.astype(LOW)
    pack_b, inputs, normed_1, order = tick([flow_a], (pack_b, inputs, normed_1, order))

    upstream_low = mm(grad_out, order).astype(LOW)
    lanes = jnp.arange(LANES, dtype=jnp.int32)
    half = HEAD_SIZE // 2
    frequency = ROPE_BASE ** (-(lanes % half).astype(F32) / half)
    positions = core * rows + jnp.arange(rows, dtype=jnp.int32)
    angles = positions.astype(F32)[:, None] * frequency[None, :]
    cosine = jnp.cos(angles)
    sine = jnp.sin(angles) * jnp.where(lanes % HEAD_SIZE < half, -1.0, 1.0)[None, :]
    heads = (jnp.arange(LANES)[:, None] == jnp.arange(INNER)[None, :] // HP).astype(LOW)
    taps = jnp.concatenate([conv_w, conv_b[None], jnp.zeros((3, CONV), F32)], axis=0)
    skip = jnp.repeat(d_skip, HP)[None, :]
    gain_s = ssm_gain[None, :]
    upstream_low, pack_b, pack_c, pack_d, cosine, sine, heads, taps, skip = tick(
        [flow_a], (upstream_low, pack_b, pack_c, pack_d, cosine, sine, heads, taps, skip)
    )
    flow_b = gather_flow([pack_b], 1024)
    flow_c = gather_flow(pack_c, 2048)
    pack_d = tick([flow_a, flow_b], pack_d)
    pack_d = tick([flow_a, flow_b, flow_c], pack_d)
    normed_1, pack_d = tick([flow_a, flow_b], (normed_1, pack_d))
    full_a = result(flow_a)
    flow_d = gather_flow([pack_d], 1024)

    proj = project(normed_1, full_a, 1408)
    proj = tick([flow_b, flow_c], proj)
    conv_low = proj[:, conv_at:dt_at].astype(LOW)
    dt_raw = proj[:, dt_at:q_at]
    k_raw = proj[:, k_at:v_at]
    k_low = (k_raw * cosine + swap_halves(k_raw) * sine).astype(LOW)
    kv = lax.all_gather(
        jnp.concatenate([k_low, proj[:, v_at:].astype(LOW)], axis=1), "seq", axis=0, tiled=True
    )
    halo = from_behind(conv_low[rows - 8 :], "seq", 1).astype(F32)
    step = jax.nn.softplus(dt_raw[:, :NH_SSM] + dt_bias[None, :])
    rate = jnp.exp(a_log)[None, :]
    log_decay = -step * rate
    lower = (jnp.arange(BLOCK)[:, None] >= jnp.arange(BLOCK)[None, :]).astype(F32)
    pad = ((0, 0), (0, LANES - NH_SSM))
    step_pad = jnp.pad(step, pad)
    run = jnp.einsum(
        "ts,ksh->kth", lower, jnp.pad(log_decay, pad).reshape(blocks, BLOCK, LANES), precision=HIGH
    )
    runt = jnp.swapaxes(run, 1, 2).reshape(rows, LANES)
    whole_decay = jnp.exp(jnp.sum(run[:, BLOCK - 1, :NH_SSM], axis=0))
    decay_wide = jnp.repeat(whole_decay, HP)[None, :]
    run = run.reshape(rows, LANES)
    pre, end_state = mixer_states(conv_low, halo, taps, step_pad, run, heads)
    kv, pre, end_state, proj = tick([flow_b, flow_c, flow_d], (kv, pre, end_state, proj))
    full_b = result(flow_b)

    incoming = jnp.zeros_like(end_state)
    for _ in range(seqs - 1):
        incoming = from_behind((end_state + decay_wide * incoming).astype(LOW), "seq", 1).astype(F32)
    start = (core * rows).astype(jnp.int32)[None]
    attended, q_low, norms = attend(start, proj, q_at, cosine, sine, kv)
    incoming, attended, proj = tick([flow_c, flow_d], (incoming, attended, proj))

    ssm_low, y, s_in, s_out = mixer_forward(
        pre, step_pad, run, runt, incoming, proj, gain_s, skip, heads
    )
    both = jnp.concatenate([ssm_low, attended], axis=1)
    both, y, s_in, s_out = tick([flow_c, flow_d], (both, y, s_in, s_out))
    full_c = result(flow_c)

    mid = inputs.astype(F32) + out_of([(both, full_b)])
    normed_2 = rms_gain(mid, gain_2).astype(LOW)
    mid, normed_2 = tick([flow_d], (mid, normed_2))

    gate_low, up_low, act = feed_forward(normed_2, full_c, 512)
    hidden = act.shape[1]
    act, gate_low, up_low = tick([flow_d], (act, gate_low, up_low))
    full_d = result(flow_d)

    sum_d = reduce_flow(upstream_low, act, 1024, 512)
    g_gate_up = feed_back(upstream_low, full_d, gate_low, up_low, 512)
    g_gate_up, act = tick([sum_d], (g_gate_up, act))

    sum_c = reduce_flow(normed_2, g_gate_up, 2048, 512)
    g_n2 = out_of(
        [(g_gate_up[0], [w[:, :hidden] for w in full_c]), (g_gate_up[1], [w[:, hidden:] for w in full_c])]
    )
    upstream = upstream_low.astype(F32)
    g_add, g_gain_2 = rms_back(g_n2, mid, gain_2)
    g_mid = upstream + g_add
    g_low = g_mid.astype(LOW)
    g_low, g_mid = tick([sum_d, sum_c], (g_low, g_mid))

    sum_b = reduce_flow(g_low, both, 1024, 512)
    g_both = project(g_low, full_b, 512)
    gy, gz, gate_sums, first_grad = gate_back(g_both, y, pre, proj, run, gain_s, skip, heads)
    gy, gz, first_grad, g_both = tick([sum_d, sum_b], (gy, gz, first_grad, g_both))

    later = jnp.zeros_like(first_grad)
    for _ in range(seqs - 1):
        later = from_behind((first_grad + decay_wide * later).astype(LOW), "seq", -1).astype(F32)
    out_perm = (mid + out_of([(act, full_d)])).astype(LOW)
    out_hidden = mm_nt(out_perm, order).astype(LOW)
    later, out_hidden = tick([sum_d, sum_c], (later, out_hidden))

    mixed = mixer_back(
        gy, y, pre, step_pad, run, runt, later, s_in, s_out, conv_low, halo, taps, skip, heads
    )
    mixed = tick([sum_d, sum_c, sum_b], mixed)
    g_conv, g_tail, rim, g_step, g_run, g_end, g_taps = mixed

    rim_back = jnp.concatenate(
        [
            sum(
                conv_w[j][None] * rim[t + KCONV - 1 - j : t + KCONV - j]
                for j in range(KCONV)
                if t + KCONV - 1 - j >= 0
            )
            for t in range(1 - KCONV, 0)
        ],
        axis=0,
    )
    rim_back = from_behind(rim_back, "seq", -1)
    tail = jnp.concatenate([g_tail[: 9 - KCONV], g_tail[9 - KCONV :] + rim_back], axis=0).astype(LOW)
    g_conv = lax.dynamic_update_slice(g_conv, tail, (rows - 8, 0))
    g_log = jnp.einsum("ts,kth->ksh", lower, g_run.reshape(blocks, BLOCK, LANES), precision=HIGH)
    g_log = (g_log + g_end[:, 0:1, :]).reshape(rows, LANES)[:, :NH_SSM]
    g_step = g_step[:, :NH_SSM] - g_log * rate
    g_dt = g_step * jax.nn.sigmoid(dt_raw[:, :NH_SSM] + dt_bias[None, :])
    g_a_log = jnp.sum(g_log * log_decay, axis=0)
    g_dt_bias = jnp.sum(g_dt, axis=0)
    g_second = jnp.concatenate([gz, g_conv, jnp.pad(g_dt, pad).astype(LOW)], axis=1)
    sum_a2 = reduce_flow(normed_1, g_second, 1920, 384)
    g_n1 = out_of([(g_second, [w[:, :q_at] for w in full_a])])
    g_n1, g_both = tick([sum_c, sum_b, sum_a2], (g_n1, g_both))

    g_q, g_kv = attend_back(start, g_both, INNER, q_low, cosine, sine, kv, norms)
    g_q, g_kv = tick([sum_c, sum_b, sum_a2], (g_q, g_kv))

    own_kv = lax.dynamic_slice_in_dim(g_kv, core * rows, rows, 0)
    for shift in range(1, seqs):
        part = lax.dynamic_slice_in_dim(g_kv, ((core + shift) % seqs) * rows, rows, 0).astype(LOW)
        own_kv = own_kv + shifted(part, "seq", shift).astype(F32)
    g_k = own_kv[:, :LANES]
    g_k_low = (g_k * cosine - swap_halves(g_k) * sine).astype(LOW)
    g_first = jnp.concatenate([g_q, g_k_low, own_kv[:, LANES:].astype(LOW)], axis=1)
    g_first, g_n1 = tick([sum_b, sum_a2], (g_first, g_n1))

    sum_a1 = reduce_flow(normed_1, g_first, 384, 384)
    out_1 = finish_flow(
        jnp.concatenate([result(sum_d), result(sum_c), result(sum_b)], axis=1), 4096,
        [(0, hidden, True), (hidden, hidden, False), (2 * hidden, hidden, False), (3 * hidden, INNER, True),
         (3 * hidden + INNER, 512, True)],
    )
    g_n1 = g_n1 + out_of([(g_first, [w[:, q_at:] for w in full_a])])
    g_add, g_gain_1 = rms_back(g_n1, inputs.astype(F32), gain_1)
    g_hidden = g_mid + g_add
    top, rest = halves(g_hidden)
    top, rest, g_gain_1 = tick([sum_a2, sum_a1, out_1], (top, rest, g_gain_1))

    g_gains = jnp.dot(
        jnp.concatenate([g_gain_1, g_gain_2, jnp.zeros((6, width), F32)], axis=0),
        order.astype(F32).T, precision=HIGH,
    )
    g_skip = gate_sums[1].reshape(NH_SSM, HP).sum(axis=1)
    small = jnp.concatenate(
        [g_gains[:2].reshape(-1), g_taps[: KCONV + 1].reshape(-1), gate_sums[0], g_dt_bias, g_a_log, g_skip,
         jnp.zeros((LANES - 3 * NH_SSM,), F32)]
    )
    grad_hidden = mm_nt(top, order) + mm_nt(rest, order)
    grad_hidden, small = tick([sum_a2, sum_a1, out_1], (grad_hidden, small))

    total = Flow(summing(small.reshape(-1, LANES)))
    early = result(out_1)
    while sum_a2.pending or sum_a1.pending:
        grad_hidden, early = tick([sum_a2, sum_a1, total], (grad_hidden, early))
    out_2 = finish_flow(
        jnp.concatenate([result(sum_a2), result(sum_a1)], axis=1), 2176,
        [(0, INNER, False), (conv_at, CONV, False), (dt_at, NH_SSM, False), (q_at, 512, False), (k_at, LANES, False),
         (v_at, LANES, False)],
    )
    while out_2.pending or total.pending:
        grad_hidden, early = tick([out_2, total], (grad_hidden, early))
    o_down, o_gate, o_up, o_mix, o_att = early
    o_z, o_conv, o_dt, o_q, o_k, o_v = result(out_2)
    small = result(total).reshape(-1)
    sizes = [width, width, KCONV * CONV, CONV, INNER, NH_SSM, NH_SSM, NH_SSM]
    starts = [sum(sizes[:k]) for k in range(len(sizes))]
    out_gain_1, out_gain_2, out_conv_w, out_conv_b, out_gain_s, out_dt_bias, out_a_log, out_skip = (
        small[at : at + size] for at, size in zip(starts, sizes)
    )
    return (
        out_hidden, grad_hidden, out_gain_1, o_z, o_conv, o_dt, out_conv_w.reshape(KCONV, CONV), out_conv_b,
        out_dt_bias, out_a_log, out_skip, out_gain_s, o_mix, o_q, o_k, o_v, o_att, out_gain_2, o_gate, o_up, o_down,
    )


def solution(mesh):
    tokens = P(("rep", "fsdp", "seq"), None)
    wide, tall, same = P(("fsdp", "seq"), None), P(None, ("fsdp", "seq")), P()
    return jax.shard_map(
        body,
        mesh=mesh,
        in_specs=(
            tokens, same, wide, wide, wide, same, same, same, same, same, same, tall,
            wide, wide, wide, tall, same, wide, wide, tall, tokens,
        ),
        out_specs=(
            tokens, tokens, same, wide, wide, wide, same, same, same, same, same, same, tall,
            wide, wide, wide, tall, same, wide, wide, tall,
        ),
        check_vma=False,
    )
```

```python
import functools

import jax
import jax.numpy as jnp
from jax import lax
from jax.experimental import pallas as pl
from jax.experimental.pallas import tpu as pltpu
from jax.sharding import PartitionSpec as P

NH_SSM = 24
HP = 64
NS = 128
KCONV = 4
QUERY_HEADS = 8
KEY_VALUE_HEADS = 2
HEAD_SIZE = 64
BLOCK = 128
INNER = NH_SSM * HP
CONV = INNER + 2 * NS
LANES = 128
PAIRS = NH_SSM // 2

HIGH = lax.Precision.HIGHEST
EPS = 1e-06
ROPE_BASE = 10000.0
SCALE = HEAD_SIZE ** (-0.5)
LOW = jnp.bfloat16
F32 = jnp.float32


def mm(a, b):
    return jnp.dot(a, b, preferred_element_type=F32)


def mm_nt(a, b):
    return lax.dot_general(a, b, (((1,), (1,)), ((), ())), preferred_element_type=F32)


def mm_tn(a, b):
    return lax.dot_general(a, b, (((0,), (0,)), ((), ())), preferred_element_type=F32)


def halves(v):
    top = v.astype(LOW)
    return top, (v - top.astype(F32)).astype(LOW)


def spread(v, heads):
    top, rest = halves(v)
    return mm(top, heads) + mm(rest, heads)


def gather_heads(v, heads):
    top, rest = halves(v)
    return mm_nt(top, heads) + mm_nt(rest, heads)


def lane_halves(shape):
    lane = lax.broadcasted_iota(jnp.int32, shape, len(shape) - 1)
    return lane % LANES < HP


def stacked(pair, left):
    zero = jnp.zeros_like(pair)
    return jnp.concatenate([jnp.where(left, pair, zero), jnp.where(left, zero, pair)], axis=0)


def states_kernel(conv_ref, halo_ref, taps_ref, step_ref, run_ref, heads_ref, pre_ref, end_ref, ext):
    block = pl.program_id(0)

    @pl.when(block == 0)
    def _():
        ext[0:8, :] = halo_ref[...]
        end_ref[...] = jnp.zeros_like(end_ref)

    @pl.when(block > 0)
    def _():
        ext[0:8, :] = ext[BLOCK : BLOCK + 8, :]

    ext[8 : BLOCK + 8, :] = conv_ref[...].astype(F32)
    pre = taps_ref[KCONV : KCONV + 1, :] + jnp.zeros((BLOCK, CONV), F32)
    for j in range(KCONV):
        pre = pre + taps_ref[j : j + 1, :] * ext[5 + j : 5 + j + BLOCK, :]
    pre_ref[...] = pre
    heads = heads_ref[...]
    run = run_ref[...]
    last = run[BLOCK - 1 : BLOCK, :]
    tail = jnp.exp(last - run) * step_ref[...]
    wide = spread(jnp.concatenate([tail, jnp.broadcast_to(jnp.exp(last), (8, LANES))], axis=0), heads)
    inner = pre[:, :INNER]
    x = inner * jax.nn.sigmoid(inner)
    bp = pre[:, INNER : INNER + NS]
    b_low = (bp * jax.nn.sigmoid(bp)).T.astype(LOW)
    weighted = (x * wide[:BLOCK]).astype(LOW)
    end_ref[...] = end_ref[...] * wide[BLOCK : BLOCK + 1] + mm(b_low, weighted)


def mixer_kernel(
    pre_ref, step_ref, run_ref, runt_ref, start_ref, z_ref, gain_ref, skip_ref, heads_ref,
    out_ref, y_ref, sin_ref, sout_ref, state,
):
    block = pl.program_id(0)

    @pl.when(block == 0)
    def _():
        state[...] = start_ref[...]

    heads = heads_ref[...]
    run = run_ref[...]
    runt = runt_ref[...]
    step = step_ref[...]
    pre = pre_ref[...]
    act = pre * jax.nn.sigmoid(pre)
    x = act[:, :INNER]
    b = act[:, INNER : INNER + NS]
    c_low = act[:, INNER + NS :].astype(LOW)
    last = run[BLOCK - 1 : BLOCK, :]
    wide = spread(
        jnp.concatenate(
            [
                step,
                jnp.exp(run),
                jnp.exp(last - run) * step,
                jnp.broadcast_to(jnp.exp(last), (8, LANES)),
            ],
            axis=0,
        ),
        heads,
    )
    x_step = (x * wide[:BLOCK]).astype(LOW)
    old = state[...]
    old_low = old.astype(LOW)
    sin_ref[0] = old_low
    carried = mm(c_low, old_low) * wide[BLOCK : 2 * BLOCK]
    weighted = (x * wide[2 * BLOCK : 3 * BLOCK]).astype(LOW)
    new = old * wide[3 * BLOCK : 3 * BLOCK + 1] + mm(b.T.astype(LOW), weighted)
    state[...] = new
    sout_ref[0] = new.astype(LOW)
    cb = mm_nt(c_low, b.astype(LOW))
    rows = lax.broadcasted_iota(jnp.int32, (BLOCK, BLOCK), 0)
    cols = lax.broadcasted_iota(jnp.int32, (BLOCK, BLOCK), 1)
    causal = rows >= cols
    left = lane_halves((BLOCK, LANES))
    parts = []
    for p in range(PAIRS):
        mixes = []
        for h in (2 * p, 2 * p + 1):
            gap = run[:, h : h + 1] - runt[h : h + 1, :]
            mixes.append((jnp.exp(jnp.where(causal, gap, -1e30)) * cb).astype(LOW))
        pair = x_step[:, p * LANES : (p + 1) * LANES]
        parts.append(mm(jnp.concatenate(mixes, axis=1), stacked(pair, left)))
    y = jnp.concatenate(parts, axis=1) + carried
    y_ref[...] = y
    z = z_ref[...]
    gated = (y + skip_ref[...] * x) * (z * jax.nn.sigmoid(z))
    inv = lax.rsqrt(jnp.mean(gated * gated, axis=-1, keepdims=True) + EPS)
    out_ref[...] = (gated * inv * gain_ref[...]).astype(LOW)


def gate_back_kernel(
    g_ref, y_ref, pre_ref, z_ref, run_ref, gain_ref, skip_ref, heads_ref,
    gy_ref, gz_ref, sums_ref, first_ref,
):
    @pl.when(pl.program_id(0) == 0)
    def _():
        sums_ref[...] = jnp.zeros_like(sums_ref)
        first_ref[...] = jnp.zeros_like(first_ref)

    heads = heads_ref[...]
    run = run_ref[...]
    last = run[BLOCK - 1 : BLOCK, :]
    wide = spread(
        jnp.concatenate([jnp.exp(run), jnp.broadcast_to(jnp.exp(last), (8, LANES))], axis=0), heads
    )
    inner = pre_ref[:, :INNER]
    x = inner * jax.nn.sigmoid(inner)
    cp = pre_ref[:, INNER + NS :]
    c = cp * jax.nn.sigmoid(cp)
    y = y_ref[...] + skip_ref[...] * x
    z = z_ref[...]
    sig = jax.nn.sigmoid(z)
    swish = z * sig
    gated = y * swish
    inv = lax.rsqrt(jnp.mean(gated * gated, axis=-1, keepdims=True) + EPS)
    g = g_ref[...]
    gg = g * gain_ref[...]
    mean = jnp.mean(gg * gated, axis=-1, keepdims=True)
    g_gated = gg * inv - gated * (inv * inv * inv * mean)
    g_y = g_gated * swish
    gz_ref[...] = (g_gated * y * (sig + swish * (1.0 - sig))).astype(LOW)
    gy_ref[...] = g_y.astype(LOW)
    sums_ref[0:1, :] += jnp.sum(g * gated * inv, axis=0, keepdims=True)
    sums_ref[1:2, :] += jnp.sum(g_y * x, axis=0, keepdims=True)
    scaled = (g_y * wide[:BLOCK]).astype(LOW)
    first_ref[...] = first_ref[...] * wide[BLOCK : BLOCK + 1] + mm(c.T.astype(LOW), scaled)


def mixer_back_kernel(
    gy_ref, y_ref, pre_ref, step_ref, run_ref, runt_ref, later_ref, sin_ref, sout_ref,
    conv_ref, before_ref, halo_ref, taps_ref, skip_ref, heads_ref,
    gconv_ref, gtail_ref, rim_ref, gstep_ref, grun_ref, gend_ref, gtaps_ref,
    grad_state, ext, dext,
):
    index = pl.program_id(0)
    count = pl.num_programs(0)

    @pl.when(index == 0)
    def _():
        grad_state[...] = later_ref[...]
        gtaps_ref[...] = jnp.zeros_like(gtaps_ref)
        dext[BLOCK : BLOCK + 8, :] = jnp.zeros((8, CONV), F32)

    @pl.when(index > 0)
    def _():
        dext[BLOCK : BLOCK + 8, :] = dext[0:8, :]

    heads = heads_ref[...]
    run = run_ref[...]
    runt = runt_ref[...]
    step = step_ref[...]
    pre = pre_ref[...]
    sig = jax.nn.sigmoid(pre)
    act = pre * sig
    x = act[:, :INNER]
    b = act[:, INNER : INNER + NS]
    c = act[:, INNER + NS :]
    b_low = b.astype(LOW)
    c_low = c.astype(LOW)
    last = run[BLOCK - 1 : BLOCK, :]
    wide = spread(
        jnp.concatenate(
            [step, jnp.exp(run), jnp.exp(last - run), jnp.broadcast_to(jnp.exp(last), (8, LANES))],
            axis=0,
        ),
        heads,
    )
    step_wide = wide[:BLOCK]
    tail_wide = wide[2 * BLOCK : 3 * BLOCK]
    gy_low = gy_ref[...]
    gy = gy_low.astype(F32)
    x_step = (x * step_wide).astype(LOW)
    later = grad_state[...]
    later_low = later.astype(LOW)
    scaled = (gy * wide[BLOCK : 2 * BLOCK]).astype(LOW)
    weighted = (x * (step_wide * tail_wide)).astype(LOW)
    grad_b = mm_nt(weighted, later_low)
    grad_c = mm_nt(scaled, sin_ref[0])
    from_state = mm(b_low, later_low) * tail_wide
    grad_state[...] = later * wide[3 * BLOCK : 3 * BLOCK + 1] + mm(c.T.astype(LOW), scaled)
    ends = jnp.sum(later * sout_ref[0].astype(F32), axis=0, keepdims=True)
    gend_ref[0] = gather_heads(jnp.broadcast_to(ends, (8, INNER)), heads)
    cbt = mm_nt(b_low, c_low)
    rows = lax.broadcasted_iota(jnp.int32, (BLOCK, BLOCK), 0)
    cols = lax.broadcasted_iota(jnp.int32, (BLOCK, BLOCK), 1)
    left = lane_halves((BLOCK, LANES))
    parts = []
    grad_cb = jnp.zeros((BLOCK, BLOCK), F32)
    for p in range(PAIRS):
        lanes = slice(p * LANES, (p + 1) * LANES)
        gy_stack = stacked(gy_low[:, lanes], left)
        products = mm_nt(gy_stack, x_step[:, lanes])
        mixes = []
        for k, h in enumerate((2 * p, 2 * p + 1)):
            column = jnp.broadcast_to(run[:, h : h + 1], (BLOCK, BLOCK))
            gap = column - runt[h : h + 1, :]
            decay = jnp.exp(jnp.where(rows >= cols, gap, -1e30))
            grad_cb = grad_cb + products[k * BLOCK : (k + 1) * BLOCK] * decay
            decay_t = jnp.exp(jnp.where(cols >= rows, -gap, -1e30))
            mixes.append((decay_t * cbt).astype(LOW))
        parts.append(mm(jnp.concatenate(mixes, axis=1), gy_stack))
    u = jnp.concatenate(parts, axis=1) + from_state
    both = gather_heads(
        jnp.concatenate([gy * y_ref[...], x * u], axis=0), heads
    )
    gstep_ref[...] = both[BLOCK:]
    grun_ref[...] = both[:BLOCK] - step * both[BLOCK:]
    grad_cb_low = grad_cb.astype(LOW)
    grad_c = grad_c + mm(grad_cb_low, b_low)
    grad_b = grad_b + mm(grad_cb.T.astype(LOW), c_low)
    grad_x = u * step_wide + skip_ref[...] * gy
    dpre = jnp.concatenate([grad_x, grad_b, grad_c], axis=1) * (sig + act * (1.0 - sig))
    dext[0:BLOCK, :] = dpre
    k = count - 1 - index
    ext[0:8, :] = jnp.where(k == 0, halo_ref[...], before_ref[BLOCK - 16 :, :].astype(F32)[8:])
    ext[8 : BLOCK + 8, :] = conv_ref[...].astype(F32)
    total = jnp.zeros((BLOCK, CONV), F32)
    for j in range(KCONV):
        total = total + taps_ref[j : j + 1, :] * dext[KCONV - 1 - j : KCONV - 1 - j + BLOCK, :]
        gtaps_ref[j : j + 1, :] += jnp.sum(dpre * ext[5 + j : 5 + j + BLOCK, :], axis=0, keepdims=True)
    gtaps_ref[KCONV : KCONV + 1, :] += jnp.sum(dpre, axis=0, keepdims=True)
    gconv_ref[...] = total.astype(LOW)

    @pl.when(index == 0)
    def _():
        gtail_ref[...] = total[BLOCK - 8 :, :]

    rim_ref[...] = dpre[0:8, :]


def fixed(shape):
    return pl.BlockSpec(shape, lambda i: (0,) * len(shape))


def params(mib):
    return pltpu.CompilerParams(
        dimension_semantics=("arbitrary",), vmem_limit_bytes=mib * 1024 * 1024
    )


def rows_of(width):
    return pl.BlockSpec((BLOCK, width), lambda i: (i, 0))


def mixer_states(conv_low, halo, taps, step, run, heads):
    rows = conv_low.shape[0]
    return pl.pallas_call(
        states_kernel,
        grid=(rows // BLOCK,),
        in_specs=[rows_of(CONV), fixed((8, CONV)), fixed((8, CONV)), rows_of(LANES), rows_of(LANES),
                  fixed((LANES, INNER))],
        out_specs=[rows_of(CONV), fixed((NS, INNER))],
        out_shape=[jax.ShapeDtypeStruct((rows, CONV), F32), jax.ShapeDtypeStruct((NS, INNER), F32)],
        scratch_shapes=[pltpu.VMEM((BLOCK + 8, CONV), F32)],
        compiler_params=params(14),
        name="mixer_states",
    )(conv_low, halo, taps, step, run, heads)


def mixer_forward(pre, step, run, runt, start, z, gain, skip, heads):
    rows = pre.shape[0]
    count = rows // BLOCK
    state_spec = pl.BlockSpec((1, NS, INNER), lambda i: (i, 0, 0))
    return pl.pallas_call(
        mixer_kernel,
        grid=(count,),
        in_specs=[rows_of(CONV), rows_of(LANES), rows_of(LANES), rows_of(LANES), fixed((NS, INNER)),
                  rows_of(INNER), fixed((1, INNER)), fixed((1, INNER)), fixed((LANES, INNER))],
        out_specs=[rows_of(INNER), rows_of(INNER), state_spec, state_spec],
        out_shape=[
            jax.ShapeDtypeStruct((rows, INNER), LOW),
            jax.ShapeDtypeStruct((rows, INNER), F32),
            jax.ShapeDtypeStruct((count, NS, INNER), LOW),
            jax.ShapeDtypeStruct((count, NS, INNER), LOW),
        ],
        scratch_shapes=[pltpu.VMEM((NS, INNER), F32)],
        compiler_params=params(14),
        name="mixer_forward",
    )(pre, step, run, runt, start, z, gain, skip, heads)


def gate_back(g, y, pre, z, run, gain, skip, heads):
    rows = pre.shape[0]
    count = rows // BLOCK

    def back(width):
        return pl.BlockSpec((BLOCK, width), lambda i: (count - 1 - i, 0))

    return pl.pallas_call(
        gate_back_kernel,
        grid=(count,),
        in_specs=[back(INNER), back(INNER), back(CONV), back(INNER), back(LANES), fixed((1, INNER)),
                  fixed((1, INNER)), fixed((LANES, INNER))],
        out_specs=[back(INNER), back(INNER), fixed((8, INNER)), fixed((NS, INNER))],
        out_shape=[
            jax.ShapeDtypeStruct((rows, INNER), LOW),
            jax.ShapeDtypeStruct((rows, INNER), LOW),
            jax.ShapeDtypeStruct((8, INNER), F32),
            jax.ShapeDtypeStruct((NS, INNER), F32),
        ],
        compiler_params=params(14),
        name="gate_back",
    )(g, y, pre, z, run, gain, skip, heads)


def mixer_back(gy, y, pre, step, run, runt, later, s_in, s_out, conv_low, halo, taps, skip, heads):
    rows = pre.shape[0]
    count = rows // BLOCK

    def back(width):
        return pl.BlockSpec((BLOCK, width), lambda i: (count - 1 - i, 0))

    state_spec = pl.BlockSpec((1, NS, INNER), lambda i: (count - 1 - i, 0, 0))
    before = pl.BlockSpec((BLOCK, CONV), lambda i: (jnp.maximum(count - 2 - i, 0), 0))
    return pl.pallas_call(
        mixer_back_kernel,
        grid=(count,),
        in_specs=[back(INNER), back(INNER), back(CONV), back(LANES), back(LANES), back(LANES),
                  fixed((NS, INNER)), state_spec, state_spec, back(CONV), before, fixed((8, CONV)),
                  fixed((8, CONV)), fixed((1, INNER)), fixed((LANES, INNER))],
        out_specs=[back(CONV), fixed((8, CONV)), fixed((8, CONV)), back(LANES), back(LANES),
                   pl.BlockSpec((1, 8, LANES), lambda i: (count - 1 - i, 0, 0)), fixed((8, CONV))],
        out_shape=[
            jax.ShapeDtypeStruct((rows, CONV), LOW),
            jax.ShapeDtypeStruct((8, CONV), F32),
            jax.ShapeDtypeStruct((8, CONV), F32),
            jax.ShapeDtypeStruct((rows, LANES), F32),
            jax.ShapeDtypeStruct((rows, LANES), F32),
            jax.ShapeDtypeStruct((count, 8, LANES), F32),
            jax.ShapeDtypeStruct((8, CONV), F32),
        ],
        scratch_shapes=[
            pltpu.VMEM((NS, INNER), F32),
            pltpu.VMEM((BLOCK + 8, CONV), F32),
            pltpu.VMEM((BLOCK + 8, CONV), F32),
        ],
        compiler_params=params(22),
        name="mixer_back",
    )(gy, y, pre, step, run, runt, later, s_in, s_out, conv_low, conv_low, halo, taps, skip, heads)


def turned(x, cosine, sine):
    half = HEAD_SIZE // 2
    lane = lax.broadcasted_iota(jnp.int32, x.shape, 1)
    other = jnp.where(
        lane % HEAD_SIZE < half, pltpu.roll(x, LANES - half, axis=1), pltpu.roll(x, half, axis=1)
    )
    return x * cosine + other * sine


def group_keys(value, group, left):
    other = pltpu.roll(value, HEAD_SIZE, axis=1)
    return jnp.where(left == (group == 0), value, other).astype(LOW)


def group_rows(value, group):
    turned_over = value.T
    return jnp.where(group == 0, turned_over[:HEAD_SIZE], turned_over[HEAD_SIZE:]).astype(LOW)


def query_chunks(rows, keys):
    size = min(rows, 256)
    return [(slice(at, at + size), keys - rows + at + size) for at in range(0, rows, size)]


def causal_mask(first, chunk, near):
    shape = (near, chunk.stop - chunk.start)
    key_at = lax.broadcasted_iota(jnp.int32, shape, 0)
    return key_at <= lax.broadcasted_iota(jnp.int32, shape, 1) + (first + chunk.start)


def to_all_keys(value, keys):
    missing = keys - value.shape[0]
    if not missing:
        return value
    return jnp.concatenate([value, jnp.zeros((missing, value.shape[1]), F32)], axis=0)


def attend_kernel(first_ref, q_ref, cos_ref, sin_ref, kv_ref, out_ref, q_low_ref, norm_ref):
    keys, rows = kv_ref.shape[0], q_ref.shape[0]
    group = pl.program_id(0) // 2
    left = lane_halves((rows, LANES))
    q = (turned(q_ref[...], cos_ref[...], sin_ref[...]).astype(LOW) * SCALE).astype(LOW)
    q_low_ref[...] = q
    k = group_keys(kv_ref[:, :LANES].astype(F32), group, lane_halves((keys, LANES)))
    vt = group_rows(kv_ref[:, LANES:].astype(F32), group)
    zero = jnp.zeros_like(q)
    parts = []
    norm_ref[...] = jnp.zeros_like(norm_ref)
    for n in range(2):
        mine = jnp.where(left, q, zero) if n == 0 else jnp.where(left, zero, q)
        heads = []
        for chunk, near in query_chunks(rows, keys):
            seen = causal_mask(first_ref[0], chunk, near)
            scores = jnp.where(seen, mm_nt(k[:near], mine[chunk]), -1e30)
            peak = jnp.max(scores, axis=0, keepdims=True)
            raised = jnp.exp(scores - peak)
            total = jnp.sum(raised, axis=0, keepdims=True)
            probs = (raised * (1.0 / total)).astype(LOW)
            norm_ref[0, n : n + 1, chunk] = peak + jnp.log(total)
            heads.append(mm(vt[:, :near], probs))
        parts.append(jnp.concatenate(heads, axis=1))
    out_ref[...] = jnp.concatenate(parts, axis=0).T.astype(LOW)


def attend_back_kernel(
    first_ref, g_ref, q_ref, cos_ref, sin_ref, kv_ref, norm_ref, gq_ref, gkv_ref
):
    keys, rows = kv_ref.shape[0], q_ref.shape[0]
    step = pl.program_id(0)
    group = step // 2
    left = lane_halves((rows, LANES))
    key_left = lane_halves((keys, LANES))
    q = q_ref[...]
    g = g_ref[...].astype(LOW)
    k_wide = kv_ref[:, :LANES].astype(F32)
    k = group_keys(k_wide, group, key_left)
    kt = group_rows(k_wide, group)
    v = group_keys(kv_ref[:, LANES:].astype(F32), group, key_left)
    zero = jnp.zeros_like(q)
    parts = []
    gk = jnp.zeros((keys, LANES), F32)
    gv = jnp.zeros((keys, LANES), F32)
    for n in range(2):
        mine = jnp.where(left, q, zero) if n == 0 else jnp.where(left, zero, q)
        grad = jnp.where(left, g, zero) if n == 0 else jnp.where(left, zero, g)
        heads = []
        for chunk, near in query_chunks(rows, keys):
            seen = causal_mask(first_ref[0], chunk, near)
            scores = jnp.where(seen, mm_nt(k[:near], mine[chunk]), -1e30)
            probs = jnp.exp(scores - norm_ref[0, n : n + 1, chunk])
            g_probs = mm_nt(v[:near], grad[chunk])
            inner = jnp.sum(probs * g_probs, axis=0, keepdims=True)
            g_scores = (probs * (g_probs - inner)).astype(LOW)
            gk = gk + to_all_keys(mm(g_scores, mine[chunk]), keys)
            gv = gv + to_all_keys(mm(probs.astype(LOW), grad[chunk]), keys)
            heads.append(mm(kt[:, :near], g_scores))
        parts.append(jnp.concatenate(heads, axis=1))
    grad_q = jnp.concatenate(parts, axis=0).T * SCALE
    gq_ref[...] = turned(grad_q, cos_ref[...], -sin_ref[...]).astype(LOW)
    here = key_left == (group == 0)

    @pl.when(step == 0)
    def _():
        gkv_ref[...] = jnp.zeros_like(gkv_ref)

    for n, value in enumerate((gk, gv)):
        both = value + pltpu.roll(value, HEAD_SIZE, axis=1)
        gkv_ref[:, n * LANES : (n + 1) * LANES] += jnp.where(here, both, 0.0)


def attend(first, proj, q_at, cosine, sine, kv):
    rows, keys = proj.shape[0], kv.shape[0]
    count = QUERY_HEADS // 2
    column = pl.BlockSpec((rows, LANES), lambda i: (0, i))
    low = jax.ShapeDtypeStruct((rows, QUERY_HEADS * HEAD_SIZE), LOW)
    return pl.pallas_call(
        attend_kernel,
        grid=(count,),
        in_specs=[
            pl.BlockSpec(memory_space=pltpu.SMEM),
            pl.BlockSpec((rows, LANES), lambda i: (0, q_at // LANES + i)),
            fixed((rows, LANES)),
            fixed((rows, LANES)),
            fixed((keys, 2 * LANES)),
        ],
        out_specs=[column, column, pl.BlockSpec((1, 8, rows), lambda i: (i, 0, 0))],
        out_shape=[low, low, jax.ShapeDtypeStruct((count, 8, rows), F32)],
        compiler_params=params(22),
        name="attend",
    )(first, proj, cosine, sine, kv)


def attend_back(first, g, g_at, q, cosine, sine, kv, norm):
    rows, keys = q.shape[0], kv.shape[0]
    count = QUERY_HEADS // 2
    column = pl.BlockSpec((rows, LANES), lambda i: (0, i))
    return pl.pallas_call(
        attend_back_kernel,
        grid=(count,),
        in_specs=[
            pl.BlockSpec(memory_space=pltpu.SMEM),
            pl.BlockSpec((rows, LANES), lambda i: (0, g_at // LANES + i)),
            column,
            fixed((rows, LANES)),
            fixed((rows, LANES)),
            fixed((keys, 2 * LANES)),
            pl.BlockSpec((1, 8, rows), lambda i: (i, 0, 0)),
        ],
        out_specs=[column, fixed((keys, 2 * LANES))],
        out_shape=[
            jax.ShapeDtypeStruct(q.shape, LOW),
            jax.ShapeDtypeStruct((keys, 2 * LANES), F32),
        ],
        compiler_params=params(22),
        name="attend_back",
    )(first, g, q, cosine, sine, kv, norm)


def trade(value, axis, bit):
    count = lax.axis_size(axis)
    return lax.ppermute(value, axis, [(i, i ^ bit) for i in range(count)])


def shifted(value, axis, by):
    count = lax.axis_size(axis)
    return lax.ppermute(value, axis, [(i, (i + by) % count) for i in range(count)])


def from_behind(value, axis, by):
    count = lax.axis_size(axis)
    pairs = [(i, i + by) for i in range(count) if 0 <= i + by < count]
    return lax.ppermute(value, axis, pairs)


def bits_of(count, flip):
    bits = [1 << k for k in range(count.bit_length() - 1)]
    return bits[::-1] if flip else bits


class Flow:
    def __init__(self, steps):
        self.steps, self.value = steps, None
        self.pending = next(steps)

    def advance(self, arrived):
        try:
            self.pending = self.steps.send(arrived)
        except StopIteration as end:
            self.pending, self.value = [], end.value


def tick(flows, values):
    flows = [f for f in flows if f.pending]
    arrived, values = lax.optimization_barrier(([f.pending for f in flows], values))
    for flow, got in zip(flows, arrived):
        flow.advance(got)
    return values


def result(flow):
    while flow.pending:
        tick([flow], ())
    return flow.value


def sharing(own, split):
    reps = lax.axis_size("rep")
    held = [{0: own[:, :split]}, {0: own[:, split:]}]
    for bits in zip(bits_of(reps, False), bits_of(reps, True)):
        orders = [sorted(h) for h in held]
        sent = [jnp.concatenate([h[b] for b in order], axis=0) for h, order in zip(held, orders)]
        got = yield [trade(v, "rep", bit) for v, bit in zip(sent, bits)]
        for h, order, bit, value in zip(held, orders, bits, got):
            value = value.reshape(len(order), -1, value.shape[1])
            for k, b in enumerate(order):
                h[b ^ bit] = value[k]
    return [[h[b] for b in range(reps)] for h in held]


def gathering(shard, split):
    reps, depth = lax.axis_size("rep"), lax.axis_size("fsdp")
    rep = lax.axis_index("rep")
    unit = shard.shape[0] // reps
    quarters = [lax.dynamic_slice_in_dim(shard, (rep ^ b) * unit, unit, 0) for b in range(reps)]
    near = {0: quarters[0]}
    for bit in bits_of(depth, True):
        order = sorted(near)
        (got,) = yield [trade(jnp.concatenate([near[s] for s in order], axis=0), "fsdp", bit)]
        for k, s in enumerate(order):
            near[s ^ bit] = got[k * unit : (k + 1) * unit]
    shared = yield from sharing(jnp.concatenate([near[s] for s in range(1, depth)], axis=0), split)
    sides = []
    for side, columns in zip(shared, (slice(0, split), slice(split, None))):
        parts = [part for b in range(reps) for part in (quarters[b][:, columns], side[b])]
        sides.append(jnp.concatenate(parts, axis=0))
    own = jnp.concatenate(sides, axis=1)
    return [own] + (yield [trade(own, "seq", a) for a in range(1, lax.axis_size("seq"))])


def reducing(left, right, split):
    seqs, reps, depth = lax.axis_size("seq"), lax.axis_size("rep"), lax.axis_size("fsdp")
    part = left.shape[1] // seqs
    sent = [mm_tn(left[:, a * part : (a + 1) * part], right).astype(LOW) for a in range(1, seqs)]
    got = yield [trade(value, "seq", a + 1) for a, value in enumerate(sent)]
    total = mm_tn(left[:, :part], right)
    for value in got:
        total = total + value.astype(F32)
    total = total.reshape(reps, part // reps, right.shape[1])
    held = [{b: total[b, :, :split] for b in range(reps)}, {b: total[b, :, split:] for b in range(reps)}]
    for bits in zip(bits_of(reps, False), bits_of(reps, True)):
        away = [sorted(b for b in h if b & bit) for h, bit in zip(held, bits)]
        sent = [jnp.concatenate([h[b] for b in bs], axis=0).astype(LOW) for h, bs in zip(held, away)]
        got = yield [trade(v, "rep", bit) for v, bit in zip(sent, bits)]
        for n, (h, bs, bit, value) in enumerate(zip(held, away, bits, got)):
            value = value.reshape(len(bs), -1, value.shape[1])
            held[n] = {b: h[b] + value[bs.index(b ^ bit)].astype(F32) for b in h if not b & bit}
    mine = jnp.concatenate([held[0][0], held[1][0]], axis=1).reshape(depth, -1, right.shape[1])
    near = {s: mine[s] for s in range(depth)}
    for bit in bits_of(depth, False):
        away = [s for s in sorted(near) if s & bit]
        (got,) = yield [trade(jnp.stack([near[s] for s in away]).astype(LOW), "fsdp", bit)]
        near = {s: near[s] + got[away.index(s ^ bit)].astype(F32) for s in near if not s & bit}
    return near[0].astype(LOW)


def completing(own, split):
    left, right = yield from sharing(own, split)
    rep = lax.axis_index("rep")
    sides = []
    for side in (left, right):
        stack = jnp.stack(side)
        ordered = [lax.dynamic_index_in_dim(stack, rep ^ q, 0, False) for q in range(len(side))]
        sides.append(jnp.concatenate(ordered, axis=0))
    return jnp.concatenate(sides, axis=1).astype(F32)


def summing(value):
    for axis in ("seq", "rep", "fsdp"):
        count = lax.axis_size(axis)
        place = lax.axis_index(axis)
        got = yield [trade(value, axis, other) for other in range(1, count)]
        held = jnp.stack([value] + got)
        value = sum(lax.dynamic_index_in_dim(held, place ^ k, 0, False) for k in range(count))
    return value


def copied(name, scalars, arrays, outs, plan):
    def kernel(*refs):
        numbers, refs = refs[: len(scalars)], refs[len(scalars) :]
        sources, targets = refs[: len(arrays)], refs[len(arrays) :]
        for a, at, o, to in plan(numbers):
            targets[o][to] = sources[a][at]

    whole = pl.BlockSpec(memory_space=pltpu.VMEM)
    return pl.pallas_call(
        kernel,
        in_specs=[pl.BlockSpec(memory_space=pltpu.SMEM)] * len(scalars) + [whole] * len(arrays),
        out_specs=[whole] * len(outs),
        out_shape=[jax.ShapeDtypeStruct(shape, LOW) for shape in outs],
        compiler_params=pltpu.CompilerParams(vmem_limit_bytes=16 * 1024 * 1024),
        name=name,
    )(*scalars, *arrays)


def span(start, size):
    return slice(start, start + size)


def quarter(rep, b, unit):
    return pl.ds(pl.multiple_of((rep[0] ^ b) * unit, unit), unit)


def gathering_fast(shards, split):
    reps, depth = lax.axis_size("rep"), lax.axis_size("fsdp")
    rep = lax.axis_index("rep").astype(jnp.int32)[None]
    unit = shards[0].shape[0] // reps
    sizes = [w.shape[1] for w in shards]
    places = [sum(sizes[:k]) for k in range(len(sizes))]
    width, every = sum(sizes), slice(None)
    (mine,) = copied(
        "pick", [rep], shards, [(unit, width)],
        lambda n: [(k, (quarter(n[0], 0, unit), every), 0, (every, span(at, size)))
                   for k, (at, size) in enumerate(zip(places, sizes))],
    )
    (second,) = yield [trade(mine, "fsdp", 2)]
    (pair,) = copied(
        "pair", [], [mine, second], [(2 * unit, width)],
        lambda n: [(k, (every, every), 0, (span(k * unit, unit), every)) for k in range(2)],
    )
    (others,) = yield [trade(pair, "fsdp", 1)]
    rows = (depth - 1) * unit
    columns = (span(0, split), span(split, width - split))
    narrow = (split, width - split)
    first = copied(
        "split", [], [others, second], [(rows, n) for n in narrow],
        lambda n: [(k, (span(at * unit, unit), columns[o]), o, (span(s * unit, unit), every))
                   for s, (k, at) in enumerate([(0, 0), (1, 0), (0, 1)]) for o in range(2)],
    )
    one = yield [trade(first[0], "rep", 1), trade(first[1], "rep", 2)]
    joined = copied(
        "join", [], [first[0], one[0], first[1], one[1]], [(2 * rows, n) for n in narrow],
        lambda n: [(2 * o + k, (every, every), o, (span(k * rows, rows), every)) for o in range(2) for k in range(2)],
    )
    two = yield [trade(joined[0], "rep", 2), trade(joined[1], "rep", 1)]
    tall = reps * depth * unit
    pieces = [first[0], one[0], two[0], first[1], one[1], two[1]]
    found = [(0, 0, 0, 0), (1, 0, 1, 0), (2, 0, 2, 0), (2, 1, 3, 0), (3, 0, 0, 1), (4, 0, 2, 1), (5, 0, 1, 1), (5, 1, 3, 1)]

    def plan(n):
        moves = []
        for b in range(reps):
            for k, (at, size) in enumerate(zip(places, sizes)):
                moves.append((k, (quarter(n[0], b, unit), every), 0, (span(b * depth * unit, unit), span(at, size))))
        for piece, part, b, o in found:
            moves.append((len(shards) + piece, (span(part * rows, rows), every), 0,
                          (span(b * depth * unit + unit, rows), columns[o])))
        return moves

    (own,) = copied("assemble", [rep], list(shards) + pieces, [(tall, width)], plan)
    return [own] + (yield [trade(own, "seq", a) for a in range(1, lax.axis_size("seq"))])


def product(left, which, right, tile):
    if right.ndim == 2:
        right = right[None]
    tokens, width = left.shape[0], right.shape[0] * right.shape[2]
    per = right.shape[2] // tile
    part = left.shape[1] // lax.axis_size("seq")

    def kernel(left_ref, right_ref, out_ref, turned_left):
        @pl.when(pl.program_id(0) == 0)
        def _():
            turned_left[...] = left_ref[...].astype(F32).T.astype(LOW)

        out_ref[...] = mm(turned_left[...], right_ref[0]).astype(LOW)

    return pl.pallas_call(
        kernel,
        grid=(width // tile,),
        in_specs=[pl.BlockSpec((tokens, part), lambda i: (0, which)),
                  pl.BlockSpec((1, tokens, tile), lambda i: (i // per, 0, i % per))],
        out_specs=pl.BlockSpec((part, tile), lambda i: (0, i)),
        out_shape=jax.ShapeDtypeStruct((part, width), LOW),
        scratch_shapes=[pltpu.VMEM((part, tokens), LOW)],
        compiler_params=params(14),
        name="product",
    )(left, right)


def product_parts(left, right, got, split, tile):
    if right.ndim == 2:
        right = right[None]
    tokens, width = left.shape[0], right.shape[0] * right.shape[2]
    per = right.shape[2] // tile
    part = left.shape[1] // lax.axis_size("seq")
    rows = part // 4
    low_tiles = split // tile

    def kernel(left_ref, right_ref, got_ref, sent_l, kept_l, sent_r, kept_r, turned_left):
        i = pl.program_id(0)

        @pl.when(i == 0)
        def _():
            turned_left[...] = left_ref[...].astype(F32).T.astype(LOW)

        total = mm(turned_left[...], right_ref[0]) + got_ref[...].astype(F32)
        b = [total[k * rows : (k + 1) * rows] for k in range(4)]

        @pl.when(i < low_tiles)
        def _():
            sent_l[0], sent_l[1] = b[1].astype(LOW), b[3].astype(LOW)
            kept_l[0], kept_l[1] = b[0], b[2]

        @pl.when(i >= low_tiles)
        def _():
            sent_r[0], sent_r[1] = b[2].astype(LOW), b[3].astype(LOW)
            kept_r[0], kept_r[1] = b[0], b[1]

    def left_spec():
        return pl.BlockSpec((2, rows, tile), lambda i: (0, 0, jnp.minimum(i, low_tiles - 1)))

    def right_spec():
        return pl.BlockSpec((2, rows, tile), lambda i: (0, 0, jnp.maximum(i - low_tiles, 0)))

    def shape(n, kind):
        return jax.ShapeDtypeStruct((2, rows, n), kind)

    return pl.pallas_call(
        kernel,
        grid=(width // tile,),
        in_specs=[pl.BlockSpec((tokens, part), lambda i: (0, 0)),
                  pl.BlockSpec((1, tokens, tile), lambda i: (i // per, 0, i % per)),
                  pl.BlockSpec((part, tile), lambda i: (0, i))],
        out_specs=[left_spec(), left_spec(), right_spec(), right_spec()],
        out_shape=[shape(split, LOW), shape(split, F32), shape(width - split, LOW), shape(width - split, F32)],
        scratch_shapes=[pltpu.VMEM((part, tokens), LOW)],
        compiler_params=params(14),
        name="product_parts",
    )(left, right, got)


def folded(kept, got):
    rows, step = kept[0].shape[1], 32

    def kernel(kl, gl, kr, gr, sl, ol, sr, o_r):
        for k, g, sent, own in ((kl, gl, sl, ol), (kr, gr, sr, o_r)):
            own[...] = k[0] + g[0].astype(F32)
            sent[...] = (k[1] + g[1].astype(F32)).astype(LOW)

    def thick(n):
        return pl.BlockSpec((2, step, n), lambda i: (0, i, 0))

    def flat(n):
        return pl.BlockSpec((step, n), lambda i: (i, 0))

    a, b = kept[0].shape[2], kept[1].shape[2]
    return pl.pallas_call(
        kernel,
        grid=(rows // step,),
        in_specs=[thick(a), thick(a), thick(b), thick(b)],
        out_specs=[flat(a), flat(a), flat(b), flat(b)],
        out_shape=[jax.ShapeDtypeStruct((rows, n), kind) for n in (a, b) for kind in (LOW, F32)],
        compiler_params=params(14),
        name="folded",
    )(kept[0], got[0], kept[1], got[1])


def spread_depth(kept, got):
    rows, a = kept[0].shape
    unit, width = rows // 4, a + kept[1].shape[1]

    def kernel(kl, gl, kr, gr, own, sent):
        for k, g, columns in ((kl, gl, slice(0, a)), (kr, gr, slice(a, width))):
            total = k[...] + g[...].astype(F32)
            for s in range(4):
                piece, at = total[s * unit : (s + 1) * unit], slice(s // 2 * unit, (s // 2 + 1) * unit)
                if s % 2:
                    sent[at, columns] = piece.astype(LOW)
                else:
                    own[at, columns] = piece

    return pl.pallas_call(
        kernel,
        out_shape=[jax.ShapeDtypeStruct((2 * unit, width), F32), jax.ShapeDtypeStruct((2 * unit, width), LOW)],
        compiler_params=pltpu.CompilerParams(vmem_limit_bytes=16 * 1024 * 1024),
        name="spread_depth",
    )(kept[0], got[0], kept[1], got[1])


def last_fold(kept, got):
    rows, width = kept.shape
    unit = rows // 2

    def kernel(k, g, own, sent):
        own[...] = k[:unit] + g[:unit].astype(F32)
        sent[...] = (k[unit:] + g[unit:].astype(F32)).astype(LOW)

    return pl.pallas_call(
        kernel,
        out_shape=[jax.ShapeDtypeStruct((unit, width), F32), jax.ShapeDtypeStruct((unit, width), LOW)],
        compiler_params=pltpu.CompilerParams(vmem_limit_bytes=16 * 1024 * 1024),
        name="last_fold",
    )(kept, got)


def reducing_fast(left, right, split, tile):
    seqs = lax.axis_size("seq")
    wide = right.shape[-1]
    wide = next(n for n in (1152, 1024, 768, 512, 384, 128) if wide % n == 0)
    sent = [product(left, a, right, wide) for a in range(1, seqs)]
    got = yield [trade(value, "seq", a + 1) for a, value in enumerate(sent)]
    got = got[0] if seqs == 2 else sum(v.astype(F32) for v in got)
    sent_l, kept_l, sent_r, kept_r = product_parts(left, right, got, split, tile)
    got = yield [trade(sent_l, "rep", 1), trade(sent_r, "rep", 2)]
    sent_l, kept_l, sent_r, kept_r = folded((kept_l, kept_r), got)
    got = yield [trade(sent_l, "rep", 2), trade(sent_r, "rep", 1)]
    own, sent = spread_depth((kept_l, kept_r), got)
    (got,) = yield [trade(sent, "fsdp", 1)]
    own, sent = last_fold(own, got)
    (got,) = yield [trade(sent, "fsdp", 2)]
    return (own + got.astype(F32)).astype(LOW)


def finishing(own, split, layout):
    reps = lax.axis_size("rep")
    unit, width = own.shape
    sides = (own[:, :split], own[:, split:])
    one = yield [trade(sides[0], "rep", 1), trade(sides[1], "rep", 2)]
    two = yield [trade(jnp.concatenate([sides[0], one[0]], axis=0), "rep", 2),
                 trade(jnp.concatenate([sides[1], one[1]], axis=0), "rep", 1)]
    rep = lax.axis_index("rep").astype(jnp.int32)[None]

    def kernel(rep_ref, own_ref, l1, r1, l2, r2, *outs):
        r = rep_ref[0]
        sections = (
            (0, split, (own_ref[:, :split], l1[...], l2[:unit], l2[unit:])),
            (split, width - split, (own_ref[:, split:], r2[:unit], r1[...], r2[unit:])),
        )
        for (first, count, flip), out in zip(layout, outs):
            for start, size, parts in sections:
                low, high = max(first, start), min(first + count, start + size)
                if low >= high:
                    continue
                parts = [p[:, low - start : min(-(-(high - start) // LANES) * LANES, size)].astype(F32) for p in parts]
                rows = []
                for q in range(reps):
                    chosen = parts[0]
                    for b in range(1, reps):
                        chosen = jnp.where((r ^ q) == b, parts[b], chosen)
                    rows.append(chosen)
                block = jnp.concatenate(rows, axis=0)
                if flip:
                    out[low - first : high - first, :] = block.T
                else:
                    out[:, low - first : high - first] = block[:, : high - low]

    whole = pl.BlockSpec(memory_space=pltpu.VMEM)
    return pl.pallas_call(
        kernel,
        in_specs=[pl.BlockSpec(memory_space=pltpu.SMEM)] + [whole] * 5,
        out_specs=[whole] * len(layout),
        out_shape=[
            jax.ShapeDtypeStruct((count, reps * unit) if flip else (reps * unit, count), F32)
            for _, count, flip in layout
        ],
        compiler_params=pltpu.CompilerParams(vmem_limit_bytes=16 * 1024 * 1024),
        name="finishing",
    )(rep, own, one[0], one[1], two[0], two[1])


def gather_flow(shards, split):
    unit = shards[0].shape[0] // lax.axis_size("rep")
    if unit % 16 == 0 and lax.axis_size("rep") == 4 and lax.axis_size("fsdp") == 4:
        return Flow(gathering_fast(shards, split))
    return Flow(gathering(jnp.concatenate(shards, axis=1), split))


def reduce_flow(left, right, split, tile):
    unit = left.shape[1] // (lax.axis_size("rep") * lax.axis_size("fsdp") * lax.axis_size("seq"))
    if unit % 16 == 0 and lax.axis_size("rep") == 4 and lax.axis_size("fsdp") == 4:
        return Flow(reducing_fast(left, right, split, tile))
    if right.ndim == 3:
        right = jnp.concatenate(list(right), axis=1)
    return Flow(reducing(left, right, split))


def finish_flow(own, split, layout):
    def plain():
        total = yield from completing(own, split)
        pieces = [total[:, first : first + count] for first, count, _ in layout]
        return [piece.T if flip else piece for piece, (_, _, flip) in zip(pieces, layout)]

    if own.shape[0] % 16 == 0 and lax.axis_size("rep") == 4:
        return Flow(finishing(own, split, layout))
    return Flow(plain())


def summed(x, weights, part):
    return sum(mm(x[:, a * part : (a + 1) * part], w[...]) for a, w in enumerate(weights))


def project(x, weight, tile):
    rows, width, part = x.shape[0], weight[0].shape[1], weight[0].shape[0]

    def kernel(x_ref, *refs):
        refs[-1][...] = summed(x_ref, refs[:-1], part)

    return pl.pallas_call(
        kernel,
        grid=(width // tile,),
        in_specs=[fixed(x.shape)] + [pl.BlockSpec((part, tile), lambda i: (0, i))] * len(weight),
        out_specs=pl.BlockSpec((rows, tile), lambda i: (0, i)),
        out_shape=jax.ShapeDtypeStruct((rows, width), F32),
        compiler_params=params(14),
        name="project",
    )(x, *weight)


def feed_forward(x, weight, tile):
    rows, width, part = x.shape[0], weight[0].shape[1] // 2, weight[0].shape[0]
    count, steps = len(weight), width // tile

    def kernel(x_ref, *refs):
        gate = summed(x_ref, refs[:count], part)
        up = summed(x_ref, refs[count : 2 * count], part)
        gate_ref, up_ref, act_ref = refs[2 * count :]
        gate_ref[...] = gate.astype(LOW)
        up_ref[...] = up.astype(LOW)
        act_ref[...] = (gate * jax.nn.sigmoid(gate) * up).astype(LOW)

    column = pl.BlockSpec((rows, tile), lambda i: (0, i))
    return pl.pallas_call(
        kernel,
        grid=(steps,),
        in_specs=[fixed(x.shape)] + [pl.BlockSpec((part, tile), lambda i: (0, i))] * count
        + [pl.BlockSpec((part, tile), lambda i: (0, steps + i))] * count,
        out_specs=[column] * 3,
        out_shape=[jax.ShapeDtypeStruct((rows, width), LOW)] * 3,
        compiler_params=params(14),
        name="feed_forward",
    )(x, *weight, *weight)


def feed_back(g, weight, gate, up, tile):
    rows, width, part = g.shape[0], weight[0].shape[1], weight[0].shape[0]

    def kernel(g_ref, gate_ref, up_ref, *refs):
        grad = summed(g_ref, refs[:-1], part)
        value = gate_ref[...].astype(F32)
        sig = jax.nn.sigmoid(value)
        swish = value * sig
        refs[-1][0] = (grad * up_ref[...].astype(F32) * (sig + swish * (1.0 - sig))).astype(LOW)
        refs[-1][1] = (grad * swish).astype(LOW)

    column = pl.BlockSpec((rows, tile), lambda i: (0, i))
    return pl.pallas_call(
        kernel,
        grid=(width // tile,),
        in_specs=[fixed(g.shape), column, column] + [pl.BlockSpec((part, tile), lambda i: (0, i))] * len(weight),
        out_specs=pl.BlockSpec((2, rows, tile), lambda i: (0, 0, i)),
        out_shape=jax.ShapeDtypeStruct((2, rows, width), LOW),
        compiler_params=params(14),
        name="feed_back",
    )(g, gate, up, *weight)


def into(x, weight):
    part = x.shape[1] // len(weight)
    return sum(mm(x[:, a * part : (a + 1) * part], w) for a, w in enumerate(weight))


def out_of(pairs):
    count = len(pairs[0][1])
    return jnp.concatenate([sum(mm_nt(g, weight[a]) for g, weight in pairs) for a in range(count)], axis=1)


def rms_back(g, v, gain):
    r = lax.rsqrt(jnp.mean(v * v, axis=-1, keepdims=True) + EPS)
    scaled = g * gain
    mean = jnp.mean(scaled * v, axis=-1, keepdims=True)
    return r * scaled - v * (r * r * r * mean), jnp.sum(g * v * r, axis=0, keepdims=True)


def rms_gain(v, gain):
    return v * lax.rsqrt(jnp.mean(v * v, axis=-1, keepdims=True) + EPS) * gain


def swap_halves(x):
    half = HEAD_SIZE // 2
    pieces = []
    for start in range(0, x.shape[1], HEAD_SIZE):
        pieces += [x[:, start + half : start + HEAD_SIZE], x[:, start : start + half]]
    return jnp.concatenate(pieces, axis=1)


def body(
    hidden_in, norm1_gain, w_z, w_xbc, w_dt, conv_w, conv_b, dt_bias, a_log, d_skip, ssm_gain, w_ssm_out,
    w_q, key_weight, value_weight, w_o, norm2_gain, w_gate, w_up, w_down, grad_out,
):
    rows, width = hidden_in.shape
    seqs, reps, depth = lax.axis_size("seq"), lax.axis_size("rep"), lax.axis_size("fsdp")
    core, rep, deep = lax.axis_index("seq"), lax.axis_index("rep"), lax.axis_index("fsdp")
    shard = w_z.shape[0]
    unit = shard // reps
    blocks = rows // BLOCK

    place = jnp.arange(width, dtype=jnp.int32)
    u, s = place % unit, place // unit % depth
    b, a = place // (unit * depth) % reps, place // (unit * depth * reps)
    source = (((deep ^ s) * seqs + (core ^ a)) * reps + (rep ^ b)) * unit + u
    order = (place[:, None] == source[None, :]).astype(LOW)

    pack_a = [w_z, w_xbc, jnp.pad(w_dt, ((0, 0), (0, LANES - NH_SSM))), w_q, key_weight, value_weight]
    conv_at, dt_at, q_at = INNER, INNER + CONV, INNER + CONV + LANES
    k_at, v_at = q_at + 512, q_at + 640
    flow_a = gather_flow(pack_a, 2176)
    pack_b = jnp.concatenate([w_ssm_out, w_o], axis=0).T
    pack_c = [w_gate, w_up]
    pack_d = w_down.T
    gains = jnp.dot(
        jnp.concatenate([norm1_gain[None], norm2_gain[None], jnp.zeros((6, width), F32)], axis=0),
        order.astype(F32), precision=HIGH,
    )
    gain_1, gain_2 = gains[0:1], gains[1:2]
    inputs = mm(hidden_in, order)
    normed_1 = rms_gain(inputs, gain_1).astype(LOW)
    inputs = inputs.astype(LOW)
    pack_b, inputs, normed_1, order = tick([flow_a], (pack_b, inputs, normed_1, order))

    upstream_low = mm(grad_out, order).astype(LOW)
    lanes = jnp.arange(LANES, dtype=jnp.int32)
    half = HEAD_SIZE // 2
    frequency = ROPE_BASE ** (-(lanes % half).astype(F32) / half)
    positions = core * rows + jnp.arange(rows, dtype=jnp.int32)
    angles = positions.astype(F32)[:, None] * frequency[None, :]
    cosine = jnp.cos(angles)
    sine = jnp.sin(angles) * jnp.where(lanes % HEAD_SIZE < half, -1.0, 1.0)[None, :]
    heads = (jnp.arange(LANES)[:, None] == jnp.arange(INNER)[None, :] // HP).astype(LOW)
    taps = jnp.concatenate([conv_w, conv_b[None], jnp.zeros((3, CONV), F32)], axis=0)
    skip = jnp.repeat(d_skip, HP)[None, :]
    gain_s = ssm_gain[None, :]
    upstream_low, pack_b, pack_c, pack_d, cosine, sine, heads, taps, skip = tick(
        [flow_a], (upstream_low, pack_b, pack_c, pack_d, cosine, sine, heads, taps, skip)
    )
    flow_b = gather_flow([pack_b], 1024)
    flow_c = gather_flow(pack_c, 2048)
    pack_d = tick([flow_a, flow_b], pack_d)
    pack_d = tick([flow_a, flow_b, flow_c], pack_d)
    normed_1, pack_d = tick([flow_a, flow_b], (normed_1, pack_d))
    full_a = result(flow_a)
    flow_d = gather_flow([pack_d], 1024)

    proj = project(normed_1, full_a, 1408)
    proj = tick([flow_b, flow_c], proj)
    conv_low = proj[:, conv_at:dt_at].astype(LOW)
    dt_raw = proj[:, dt_at:q_at]
    k_raw = proj[:, k_at:v_at]
    k_low = (k_raw * cosine + swap_halves(k_raw) * sine).astype(LOW)
    kv = lax.all_gather(
        jnp.concatenate([k_low, proj[:, v_at:].astype(LOW)], axis=1), "seq", axis=0, tiled=True
    )
    halo = from_behind(conv_low[rows - 8 :], "seq", 1).astype(F32)
    step = jax.nn.softplus(dt_raw[:, :NH_SSM] + dt_bias[None, :])
    rate = jnp.exp(a_log)[None, :]
    log_decay = -step * rate
    lower = (jnp.arange(BLOCK)[:, None] >= jnp.arange(BLOCK)[None, :]).astype(F32)
    pad = ((0, 0), (0, LANES - NH_SSM))
    step_pad = jnp.pad(step, pad)
    run = jnp.einsum(
        "ts,ksh->kth", lower, jnp.pad(log_decay, pad).reshape(blocks, BLOCK, LANES), precision=HIGH
    )
    runt = jnp.swapaxes(run, 1, 2).reshape(rows, LANES)
    whole_decay = jnp.exp(jnp.sum(run[:, BLOCK - 1, :NH_SSM], axis=0))
    decay_wide = jnp.repeat(whole_decay, HP)[None, :]
    run = run.reshape(rows, LANES)
    pre, end_state = mixer_states(conv_low, halo, taps, step_pad, run, heads)
    kv, pre, end_state, proj = tick([flow_b, flow_c, flow_d], (kv, pre, end_state, proj))
    full_b = result(flow_b)

    incoming = jnp.zeros_like(end_state)
    for _ in range(seqs - 1):
        incoming = from_behind((end_state + decay_wide * incoming).astype(LOW), "seq", 1).astype(F32)
    start = (core * rows).astype(jnp.int32)[None]
    attended, q_low, norms = attend(start, proj, q_at, cosine, sine, kv)
    incoming, attended, proj = tick([flow_c, flow_d], (incoming, attended, proj))

    ssm_low, y, s_in, s_out = mixer_forward(
        pre, step_pad, run, runt, incoming, proj, gain_s, skip, heads
    )
    both = jnp.concatenate([ssm_low, attended], axis=1)
    both, y, s_in, s_out = tick([flow_c, flow_d], (both, y, s_in, s_out))
    full_c = result(flow_c)

    mid = inputs.astype(F32) + out_of([(both, full_b)])
    normed_2 = rms_gain(mid, gain_2).astype(LOW)
    mid, normed_2 = tick([flow_d], (mid, normed_2))

    gate_low, up_low, act = feed_forward(normed_2, full_c, 512)
    hidden = act.shape[1]
    act, gate_low, up_low = tick([flow_d], (act, gate_low, up_low))
    full_d = result(flow_d)

    sum_d = reduce_flow(upstream_low, act, 1024, 512)
    g_gate_up = feed_back(upstream_low, full_d, gate_low, up_low, 512)
    g_gate_up, act = tick([sum_d], (g_gate_up, act))

    sum_c = reduce_flow(normed_2, g_gate_up, 2048, 512)
    g_n2 = out_of(
        [(g_gate_up[0], [w[:, :hidden] for w in full_c]), (g_gate_up[1], [w[:, hidden:] for w in full_c])]
    )
    upstream = upstream_low.astype(F32)
    g_add, g_gain_2 = rms_back(g_n2, mid, gain_2)
    g_mid = upstream + g_add
    g_low = g_mid.astype(LOW)
    g_low, g_mid = tick([sum_d, sum_c], (g_low, g_mid))

    sum_b = reduce_flow(g_low, both, 1024, 512)
    g_both = project(g_low, full_b, 512)
    gy, gz, gate_sums, first_grad = gate_back(g_both, y, pre, proj, run, gain_s, skip, heads)
    gy, gz, first_grad, g_both = tick([sum_d, sum_b], (gy, gz, first_grad, g_both))

    later = jnp.zeros_like(first_grad)
    for _ in range(seqs - 1):
        later = from_behind((first_grad + decay_wide * later).astype(LOW), "seq", -1).astype(F32)
    out_perm = (mid + out_of([(act, full_d)])).astype(LOW)
    out_hidden = mm_nt(out_perm, order).astype(LOW)
    later, out_hidden = tick([sum_d, sum_c], (later, out_hidden))

    mixed = mixer_back(
        gy, y, pre, step_pad, run, runt, later, s_in, s_out, conv_low, halo, taps, skip, heads
    )
    mixed = tick([sum_d, sum_c, sum_b], mixed)
    g_conv, g_tail, rim, g_step, g_run, g_end, g_taps = mixed

    rim_back = jnp.concatenate(
        [
            sum(
                conv_w[j][None] * rim[t + KCONV - 1 - j : t + KCONV - j]
                for j in range(KCONV)
                if t + KCONV - 1 - j >= 0
            )
            for t in range(1 - KCONV, 0)
        ],
        axis=0,
    )
    rim_back = from_behind(rim_back, "seq", -1)
    tail = jnp.concatenate([g_tail[: 9 - KCONV], g_tail[9 - KCONV :] + rim_back], axis=0).astype(LOW)
    g_conv = lax.dynamic_update_slice(g_conv, tail, (rows - 8, 0))
    g_log = jnp.einsum("ts,kth->ksh", lower, g_run.reshape(blocks, BLOCK, LANES), precision=HIGH)
    g_log = (g_log + g_end[:, 0:1, :]).reshape(rows, LANES)[:, :NH_SSM]
    g_step = g_step[:, :NH_SSM] - g_log * rate
    g_dt = g_step * jax.nn.sigmoid(dt_raw[:, :NH_SSM] + dt_bias[None, :])
    g_a_log = jnp.sum(g_log * log_decay, axis=0)
    g_dt_bias = jnp.sum(g_dt, axis=0)
    g_second = jnp.concatenate([gz, g_conv, jnp.pad(g_dt, pad).astype(LOW)], axis=1)
    sum_a2 = reduce_flow(normed_1, g_second, 1920, 384)
    g_n1 = out_of([(g_second, [w[:, :q_at] for w in full_a])])
    g_n1, g_both = tick([sum_c, sum_b, sum_a2], (g_n1, g_both))

    g_q, g_kv = attend_back(start, g_both, INNER, q_low, cosine, sine, kv, norms)
    g_q, g_kv = tick([sum_c, sum_b, sum_a2], (g_q, g_kv))

    own_kv = lax.dynamic_slice_in_dim(g_kv, core * rows, rows, 0)
    for shift in range(1, seqs):
        part = lax.dynamic_slice_in_dim(g_kv, ((core + shift) % seqs) * rows, rows, 0).astype(LOW)
        own_kv = own_kv + shifted(part, "seq", shift).astype(F32)
    g_k = own_kv[:, :LANES]
    g_k_low = (g_k * cosine - swap_halves(g_k) * sine).astype(LOW)
    g_first = jnp.concatenate([g_q, g_k_low, own_kv[:, LANES:].astype(LOW)], axis=1)
    g_first, g_n1 = tick([sum_b, sum_a2], (g_first, g_n1))

    sum_a1 = reduce_flow(normed_1, g_first, 384, 384)
    out_1 = finish_flow(
        jnp.concatenate([result(sum_d), result(sum_c), result(sum_b)], axis=1), 4096,
        [(0, hidden, True), (hidden, hidden, False), (2 * hidden, hidden, False), (3 * hidden, INNER, True),
         (3 * hidden + INNER, 512, True)],
    )
    g_n1 = g_n1 + out_of([(g_first, [w[:, q_at:] for w in full_a])])
    g_add, g_gain_1 = rms_back(g_n1, inputs.astype(F32), gain_1)
    g_hidden = g_mid + g_add
    top, rest = halves(g_hidden)
    top, rest, g_gain_1 = tick([sum_a2, sum_a1, out_1], (top, rest, g_gain_1))

    g_gains = jnp.dot(
        jnp.concatenate([g_gain_1, g_gain_2, jnp.zeros((6, width), F32)], axis=0),
        order.astype(F32).T, precision=HIGH,
    )
    g_skip = gate_sums[1].reshape(NH_SSM, HP).sum(axis=1)
    small = jnp.concatenate(
        [g_gains[:2].reshape(-1), g_taps[: KCONV + 1].reshape(-1), gate_sums[0], g_dt_bias, g_a_log, g_skip,
         jnp.zeros((LANES - 3 * NH_SSM,), F32)]
    )
    grad_hidden = mm_nt(top, order) + mm_nt(rest, order)
    grad_hidden, small = tick([sum_a2, sum_a1, out_1], (grad_hidden, small))

    total = Flow(summing(small.reshape(-1, LANES)))
    early = result(out_1)
    while sum_a2.pending or sum_a1.pending:
        grad_hidden, early = tick([sum_a2, sum_a1, total], (grad_hidden, early))
    out_2 = finish_flow(
        jnp.concatenate([result(sum_a2), result(sum_a1)], axis=1), 2176,
        [(0, INNER, False), (conv_at, CONV, False), (dt_at, NH_SSM, False), (q_at, 512, False), (k_at, LANES, False),
         (v_at, LANES, False)],
    )
    while out_2.pending or total.pending:
        grad_hidden, early = tick([out_2, total], (grad_hidden, early))
    o_down, o_gate, o_up, o_mix, o_att = early
    o_z, o_conv, o_dt, o_q, o_k, o_v = result(out_2)
    small = result(total).reshape(-1)
    sizes = [width, width, KCONV * CONV, CONV, INNER, NH_SSM, NH_SSM, NH_SSM]
    starts = [sum(sizes[:k]) for k in range(len(sizes))]
    out_gain_1, out_gain_2, out_conv_w, out_conv_b, out_gain_s, out_dt_bias, out_a_log, out_skip = (
        small[at : at + size] for at, size in zip(starts, sizes)
    )
    return (
        out_hidden, grad_hidden, out_gain_1, o_z, o_conv, o_dt, out_conv_w.reshape(KCONV, CONV), out_conv_b,
        out_dt_bias, out_a_log, out_skip, out_gain_s, o_mix, o_q, o_k, o_v, o_att, out_gain_2, o_gate, o_up, o_down,
    )


def solution(mesh):
    tokens = P(("rep", "fsdp", "seq"), None)
    wide, tall, same = P(("fsdp", "seq"), None), P(None, ("fsdp", "seq")), P()
    return jax.shard_map(
        body,
        mesh=mesh,
        in_specs=(
            tokens, same, wide, wide, wide, same, same, same, same, same, same, tall,
            wide, wide, wide, tall, same, wide, wide, tall, tokens,
        ),
        out_specs=(
            tokens, tokens, same, wide, wide, wide, same, same, same, same, same, same, tall,
            wide, wide, wide, tall, same, wide, wide, tall,
        ),
        check_vma=False,
    )
```
